32 devices in a mesh: tok: 32 (over z, y, x, core), head: 1.
Axes of the slice: x: 2, y: 2, z: 4, core: 2. Of those that a mesh axis runs over, the one named last changes fastest.
Arguments:
- queries: bfloat16 [8192, 2560], P('tok', 'head'), may hold values from -256 to 256
- keys: bfloat16 [8192, 2560], P('tok', 'head'), may hold values from -6 to 6
- values: bfloat16 [8192, 2560], P('tok', 'head'), may hold values from -6 to 6
- rates: float32 [8192, 8], P('tok', 'head'), may hold values from 0.00022097086 to 0.0044194176
- back: int32 [8192], P('tok'), may hold values from 64 to 511
- group_end: int32 [1], replicated, may hold values from 2048 to 6143
- gate_init: float32 [8, 320, 320], P('head', None, 'tok'), may hold values from -0.3125 to 0.3125
- up_init: float32 [8, 320, 320], P('head', None, 'tok'), may hold values from -0.3125 to 0.3125
- down_init: float32 [8, 320, 320], P('head', None, 'tok'), may hold values from -0.3125 to 0.3125
- gain: float32 [2560], P('head'), may hold values from 0.5 to 1.5
Outputs:
- output: bfloat16 [8192, 2560], P('tok', 'head')
- gate_final: float32 [8, 320, 320], P('head', None, 'tok')
- up_final: float32 [8, 320, 320], P('head', None, 'tok')
- down_final: float32 [8, 320, 320], P('head', None, 'tok')
The draws below stay inside these ranges and needn't reach their ends.
All inputs are finite; a program needn't handle non-finite values.
Results may differ from the reference program's by a relative error of at most 0.0088.
Values may be sent and summed in bfloat16 or wider, within the bound.
No kernel may reach another device: no remote copies, remote signals or barrier semaphores. Data moves between devices by JAX's collectives and lax.ppermute only.
A program may use at most 128 MiB of HBM per device.

```python
import math
import jax
import jax.numpy as jnp
from jax import lax

HEADS = 8
HD = 320
FH = 320
WINDOW = 512
TOKENS = 8192


def joint_fields(key):
    base_keys = jnp.clip(jax.random.normal(jax.random.fold_in(key, 11), (TOKENS, HEADS * HD), jnp.float32), -6.0, 6.0)
    base_queries = jnp.clip(jax.random.normal(jax.random.fold_in(key, 12), (TOKENS, HEADS * HD), jnp.float32), -6.0, 6.0)
    return (base_queries, base_keys)


def draw_queries(key, part):
    queries, keys = joint_fields(key)
    return queries.astype(jnp.bfloat16)


def draw_keys(key, part):
    queries, keys = joint_fields(key)
    return keys.astype(jnp.bfloat16)


def with_ends(drawn, stream_key, low, high):
    longest = drawn.shape.index(max(drawn.shape))
    spots = []
    for shift in (0, 1):
        where = [jax.random.randint(jax.random.fold_in(stream_key, axis), (), 0, length) for axis, length in enumerate(drawn.shape)]
        where[longest] = (where[longest] + shift) % drawn.shape[longest]
        spots.append(tuple(where))
    return drawn.at[spots[0]].set(low).at[spots[1]].set(high)


def level_of(own_key, shape, shards, low, top_value):
    level = 1.0
    for dim, shards_of in shards:
        heights = jax.random.uniform(jax.random.fold_in(jax.random.fold_in(own_key, 6), dim), (shards_of,), jnp.float32, low / len(shards), top_value / len(shards))
        level = level * jnp.repeat(jnp.exp(heights), shape[dim] // shards_of).reshape((-1,) + (1,) * (len(shape) - 1 - dim))
    return level


def gaussian(key, dims, spread, most, shards=(), kind=jnp.bfloat16):
    loudness = level_of(key, dims, shards, -0.22, 0.18) if shards else 1.0
    values = jax.random.normal(key, dims, jnp.float32) * spread * loudness
    return jnp.minimum(jnp.maximum(values, -most), most).astype(kind)


def setup_inputs(seed: int = 0) -> dict:
    splits = jax.random.split(jax.random.key(seed), 11)
    queries = draw_queries(jax.random.fold_in(splits[10], 71), 0)
    keys = draw_keys(jax.random.fold_in(splits[10], 71), 0)
    values = gaussian(splits[2], (TOKENS, HEADS * HD), 1.0, 6.0, ((0, 32),))
    rates = jnp.clip(jnp.exp(math.log(0.0044194176) - 2.9957324 * jax.random.uniform(splits[3], (TOKENS, HEADS), jnp.float32) ** level_of(splits[3], (TOKENS, HEADS), ((0, 32),), -0.2, 0.2)), 0.00022097086, 0.0044194176)
    back = with_ends(jax.random.randint(splits[4], (TOKENS,), WINDOW // 8, WINDOW), jax.random.fold_in(splits[4], 1), WINDOW // 8, WINDOW - 1).astype(jnp.int32)
    group_end = jax.random.randint(splits[5], (1,), TOKENS // 4, 3 * TOKENS // 4).astype(jnp.int32)
    gate_init = gaussian(splits[6], (HEADS, HD, FH), HD ** -0.5, 0.3125, ((2, 32),), jnp.float32)
    up_init = gaussian(splits[7], (HEADS, HD, FH), HD ** -0.5, 0.3125, ((2, 32),), jnp.float32)
    down_init = gaussian(splits[8], (HEADS, FH, HD), FH ** -0.5, 0.3125, ((2, 32),), jnp.float32)
    gain = jnp.clip(1.0 + 0.1 * jax.random.normal(splits[9], (HEADS * HD,), jnp.float32), 0.5, 1.5)
    return dict(queries=queries, keys=keys, values=values, rates=rates, back=back, group_end=group_end, gate_init=gate_init, up_init=up_init, down_init=down_init, gain=gain)


def swiglu_apply(w_gate, w_up, w_down, inputs):
    pre_gate = jnp.dot(inputs, w_gate, preferred_element_type=jnp.float32)
    pre_up = jnp.dot(inputs, w_up, preferred_element_type=jnp.float32)
    hidden = (pre_gate * jax.nn.sigmoid(pre_gate) * pre_up).astype(jnp.bfloat16)
    return jnp.dot(hidden, w_down, preferred_element_type=jnp.float32)

def swiglu_grads(w_gate, w_up, w_down, key_rows, value_rows, step_rates):
    pre_gate = jnp.dot(key_rows, w_gate, preferred_element_type=jnp.float32)
    pre_up = jnp.dot(key_rows, w_up, preferred_element_type=jnp.float32)
    sigma = jax.nn.sigmoid(pre_gate)
    active = pre_gate * sigma
    hidden = (active * pre_up).astype(jnp.bfloat16)
    errors = (-step_rates[:, None] * value_rows.astype(jnp.float32)).astype(jnp.bfloat16)
    grad_down = jnp.dot(hidden.T, errors, preferred_element_type=jnp.float32)
    d_hidden = jnp.dot(errors, w_down.T, preferred_element_type=jnp.float32)
    d_gate = (d_hidden * pre_up * sigma * (1.0 + pre_gate * (1.0 - sigma))).astype(jnp.bfloat16)
    d_up = (d_hidden * active).astype(jnp.bfloat16)
    grad_gate = jnp.dot(key_rows.T, d_gate, preferred_element_type=jnp.float32)
    grad_up = jnp.dot(key_rows.T, d_up, preferred_element_type=jnp.float32)
    return (grad_gate, grad_up, grad_down)

def rescale(weight, grad):
    fresh = weight - grad
    old_norm = jnp.sqrt(lax.optimization_barrier(jnp.sum(weight * weight, axis=0, keepdims=True)))
    new_norm = jnp.sqrt(lax.optimization_barrier(jnp.sum(fresh * fresh, axis=0, keepdims=True)) + 1e-06)
    return fresh * (old_norm / new_norm)

def reference(queries, keys, values, rates, back, group_end, gate_init, up_init, down_init, gain):
    positions = jnp.arange(TOKENS, dtype=jnp.int32)
    first = positions < group_end[0]
    query3 = queries.reshape(TOKENS, HEADS, HD)
    key3 = keys.reshape(TOKENS, HEADS, HD)
    value3 = values.reshape(TOKENS, HEADS, HD)

    def one_head(items):
        q_rows, k_rows, v_rows, lr_rows, w_gate, w_up, w_down = items
        state = (w_gate, w_up, w_down)
        outs = []
        for group in range(2):
            live = first if group == 0 else jnp.logical_not(first)
            packed = tuple((w.astype(jnp.bfloat16) for w in state))
            outs.append(swiglu_apply(packed[0], packed[1], packed[2], q_rows))
            grads = swiglu_grads(packed[0], packed[1], packed[2], k_rows, v_rows, jnp.where(live, lr_rows, 0.0))
            state = tuple((rescale(w, g) for w, g in zip(state, grads)))
        mixed = jnp.where(first[:, None], outs[0], outs[1])
        return (mixed, state[0], state[1], state[2])
    mixed, gate_final, up_final, down_final = lax.map(one_head, (query3.transpose(1, 0, 2), key3.transpose(1, 0, 2), value3.transpose(1, 0, 2), rates.T, gate_init, up_init, down_init))
    mixed = mixed.transpose(1, 0, 2)
    mean_square = lax.optimization_barrier(jnp.mean(mixed * mixed, axis=(1, 2), keepdims=True))
    normed = mixed / jnp.sqrt(mean_square + 1e-06) * gain.reshape(1, HEADS, HD)
    block = math.gcd(TOKENS, 512)
    key_pad = jnp.concatenate([jnp.zeros((WINDOW, HEADS, HD), jnp.bfloat16), key3], axis=0)
    value_pad = jnp.concatenate([jnp.zeros((WINDOW, HEADS, HD), jnp.bfloat16), value3], axis=0)

    def attend(index):
        begin = (index * block).astype(jnp.int32)
        q_block = lax.dynamic_slice_in_dim(query3, begin, block, 0).astype(jnp.float32)
        k_block = lax.dynamic_slice_in_dim(key_pad, begin, block + WINDOW, 0).astype(jnp.float32)
        v_block = lax.dynamic_slice_in_dim(value_pad, begin, block + WINDOW, 0).astype(jnp.float32)
        reach = lax.dynamic_slice_in_dim(back, begin, block, 0)
        q_pos = begin + jnp.arange(block, dtype=jnp.int32)
        k_pos = begin - WINDOW + jnp.arange(block + WINDOW, dtype=jnp.int32)
        allowed = (k_pos[None, :] >= 0) & (k_pos[None, :] <= q_pos[:, None]) & (k_pos[None, :] >= q_pos[:, None] - reach[:, None])
        scores = jnp.einsum('qhd,khd->hqk', q_block, k_block) * (1.0 / math.sqrt(HD))
        scores = jnp.where(allowed[None], scores, -jnp.inf)
        top = lax.optimization_barrier(jnp.max(scores, axis=2, keepdims=True))
        weights = jnp.where(allowed[None], jnp.exp(scores - top), 0.0)
        total = lax.optimization_barrier(jnp.sum(weights, axis=2, keepdims=True))
        probs = (weights / total).astype(jnp.bfloat16).astype(jnp.float32)
        return jnp.einsum('hqk,khd->qhd', probs, v_block)
    attn = lax.map(attend, jnp.arange(TOKENS // block, dtype=jnp.int32))
    attn = attn.reshape(TOKENS, HEADS, HD)
    output = (normed + attn).astype(jnp.bfloat16).reshape(TOKENS, HEADS * HD)
    return (output, gate_final, up_final, down_final)
```

```python
import functools
import math

import jax
import jax.numpy as jnp
from jax import lax
from jax.experimental import pallas as pl
from jax.experimental.pallas import tpu as pltpu
from jax.sharding import PartitionSpec as P

WINDOW = 512
BF16 = jnp.bfloat16
F32 = jnp.float32
MIB = 1 << 20

VMEM = pl.BlockSpec(memory_space=pltpu.VMEM)
SMEM = pl.BlockSpec(memory_space=pltpu.SMEM)


def dot(lhs, rhs, lhs_dim, rhs_dim):
    return lax.dot_general(
        lhs, rhs, (((lhs_dim,), (rhs_dim,)), ((), ())), preferred_element_type=F32
    )


def call(body, info, inputs, outputs, scratch=(), flops=0, limit=32):
    moved = sum(math.prod(x.shape) * x.dtype.itemsize for x in list(inputs) + list(outputs))
    return pl.pallas_call(
        body,
        out_shape=tuple(outputs),
        in_specs=[SMEM] + [VMEM] * len(inputs),
        out_specs=tuple(VMEM for _ in outputs),
        scratch_shapes=list(scratch),
        compiler_params=pltpu.CompilerParams(vmem_limit_bytes=limit * MIB),
        cost_estimate=pl.CostEstimate(flops=flops, bytes_accessed=moved, transcendentals=0),
    )(info, *inputs)


class Plan:
    def __init__(self, rows, heads, width, cols, count):
        self.rows, self.heads, self.width, self.cols, self.count = rows, heads, width, cols, count
        self.group = heads
        self.planes = count // heads
        self.fold = 2 if cols % 2 == 0 else 1
        self.part = cols // self.fold
        self.used = 3 * self.part
        self.lines = -(-(self.used + 1) // 16) * 16
        self.wide = self.fold * width
        self.pad = -(-width // 128) * 128
        self.half = rows // 2
        self.tail = -(-WINDOW // rows)
        self.wire = (count, self.lines, self.wide)


def pack_state(plan, info, states, rates):
    def body(info_ref, gate, up, down, rate, out, lines):
        lines[...] = jnp.zeros_like(lines)
        for kind, ref in enumerate((gate, up, down)):
            for col in range(plan.cols):
                side, line = divmod(col, plan.part)
                lanes = slice(side * plan.width, (side + 1) * plan.width)
                lines[:, kind * plan.part + line, lanes] = ref[col]
        if plan.group > 1:
            high = rate[...].astype(BF16).astype(F32)
            lines[:, plan.used, 0 : plan.rows] = high
            lines[:, plan.used, plan.rows : 2 * plan.rows] = rate[...] - high
        packed = lines[...].astype(BF16)
        for plane in range(plan.planes):
            out[plane * plan.group : (plane + 1) * plan.group] = packed

    return call(
        body,
        info,
        (*states, rates),
        (jax.ShapeDtypeStruct(plan.wire, BF16),),
        [pltpu.VMEM((plan.group, plan.lines, plan.wide), F32)],
    )[0]


def update(plan, info, states, wire, send):
    def body(info_ref, gate, up, down, wire_ref, *rest):
        news, rest = rest[:3], rest[3:]
        out = rest[0] if send else None
        total, grad = rest[-2:]
        acc = wire_ref[0 : plan.group].astype(F32)
        for plane in range(1, plan.planes):
            acc += wire_ref[plane * plan.group : (plane + 1) * plan.group].astype(F32)
        total[...] = acc
        for kind, ref in enumerate((gate, up, down)):
            for col in range(plan.cols):
                side, line = divmod(col, plan.part)
                lanes = slice(side * plan.width, (side + 1) * plan.width)
                grad[col] = total[:, kind * plan.part + line, lanes]
            old = ref[...]
            fresh = old - grad[...]
            old_norm = jnp.sqrt(jnp.sum(old * old, axis=2, keepdims=True))
            new_norm = jnp.sqrt(jnp.sum(fresh * fresh, axis=2, keepdims=True) + 1e-06)
            new = fresh * (old_norm / new_norm)
            news[kind][...] = new
            if send:
                for col in range(plan.cols):
                    side, line = divmod(col, plan.part)
                    lanes = slice(side * plan.width, (side + 1) * plan.width)
                    total[:, kind * plan.part + line, lanes] = new[col]
        if send:
            packed = total[...].astype(BF16)
            for plane in range(plan.planes):
                out[plane * plan.group : (plane + 1) * plan.group] = packed

    state = jax.ShapeDtypeStruct((plan.cols, plan.heads, plan.width), F32)
    outputs = (state, state, state)
    if send:
        outputs += (jax.ShapeDtypeStruct(plan.wire, BF16),)
    return call(
        body,
        info,
        (*states, wire),
        outputs,
        [
            pltpu.VMEM((plan.group, plan.lines, plan.wide), F32),
            pltpu.VMEM((plan.cols, plan.heads, plan.width), F32),
        ],
    )


def pack_pair(plan, info, left, right, name):
    def body(info_ref, left_ref, right_ref, *outs):
        for step in range(plan.group):
            head = info_ref[0] ^ step
            lanes = pl.ds(pl.multiple_of((head >> 1) * 2 * plan.width, 128), 2 * plan.width)
            for odd in (0, 1):

                @pl.when((head & 1) == odd)
                def _():
                    own = slice(odd * plan.width, (odd + 1) * plan.width)
                    outs[step][:, 0 : plan.width] = left_ref[:, lanes][:, own]
                    outs[step][:, plan.width : 2 * plan.width] = right_ref[:, lanes][:, own]

    if plan.group == 1:
        return (jnp.concatenate([left, right], axis=1),)
    block = jax.ShapeDtypeStruct((plan.rows, 2 * plan.width), BF16)
    return call(body, info, (left, right), (block,) * plan.group)


def pack_queries(plan, info, queries, reach):
    half, width = plan.half, plan.width

    def fill(out, own, back):
        out[0:half, 0:width] = own[0:half]
        out[0:half, width : 2 * width] = own[half : 2 * half]
        high = jnp.floor(back * (1.0 / 16.0))
        line = jnp.concatenate([high, back - 16.0 * high], axis=1)
        tail = jnp.zeros((16, 2 * plan.rows), F32) + line
        out[half : half + 16, 0 : 2 * plan.rows] = tail.astype(BF16)
        out[half : half + 16, 2 * plan.rows :] = jnp.zeros((16, 2 * (width - plan.rows)), BF16)

    def body(info_ref, query_ref, back_ref, *outs):
        back = back_ref[...]
        if plan.group == 1:
            fill(outs[0], query_ref[...], back)
            return
        for step in range(plan.group):
            head = info_ref[0] ^ step
            lanes = pl.ds(pl.multiple_of((head >> 1) * 2 * width, 128), 2 * width)
            for odd in (0, 1):

                @pl.when((head & 1) == odd)
                def _():
                    own = slice(odd * width, (odd + 1) * width)
                    fill(outs[step], query_ref[:, lanes][:, own], back)

    block = jax.ShapeDtypeStruct((half + 16, 2 * width), BF16)
    return call(body, info, (queries, reach), (block,) * plan.group)


def exchange(plan, blocks):
    moved = [blocks[0]]
    for step in range(1, plan.group):
        pairs = [(source, source ^ step) for source in range(plan.count)]
        moved.append(lax.ppermute(blocks[step], "tok", pairs))
    return moved


def unfold(plan, ref):
    half, width = plan.half, plan.width
    return jnp.concatenate([ref[0:half, 0:width], ref[0:half, width : 2 * width]], axis=0)


def fold_into(plan, ref, value):
    half, width = plan.half, plan.width
    ref[:, 0:width] = value[0:half]
    ref[:, width : 2 * width] = value[half : 2 * half]


def column(row):
    return jnp.swapaxes(jnp.broadcast_to(row, (8, row.shape[1])), 0, 1)[:, 0:1]


def block_start(plan, info_ref, step):
    return info_ref[1] + (info_ref[0] ^ step) * plan.rows


def gradients(plan, info, wire, blocks, rates, number):
    width, pad, rows = plan.width, plan.pad, plan.rows
    first_call = number == 0 and plan.group > 1

    def body(info_ref, wire_ref, rate_ref, *rest):
        kv, rest = rest[: plan.group], rest[plan.group :]
        out, both_ref, down_ref = rest[:3]
        halo = rest[3] if first_call else None
        rate_out = rest[4] if first_call else None
        wide, acc_both, acc_down, lines = rest[-4:]
        for owner in range(plan.count):
            chunk = wire_ref[owner].astype(F32)
            for kind in range(3):
                for side in range(plan.fold):
                    begin = kind * pad + owner * plan.cols + side * plan.part
                    wide[begin : begin + plan.part, :] = chunk[
                        kind * plan.part : (kind + 1) * plan.part,
                        side * width : (side + 1) * width,
                    ]
        if pad > width:
            for kind in range(2):
                wide[kind * pad + width : (kind + 1) * pad, :] = jnp.zeros((pad - width, width), F32)
        both_ref[...] = wide[0 : 2 * pad, :].astype(BF16)
        down_ref[...] = wide[2 * pad : 2 * pad + width, :].astype(BF16)
        acc_both[...] = jnp.zeros_like(acc_both)
        acc_down[...] = jnp.zeros_like(acc_down)
        for step in range(plan.group):
            block = info_ref[0] ^ step
            start = info_ref[1] + block * rows
            if first_call:
                line = wire_ref[info_ref[3] + block].astype(F32)
                rate_row = (
                    line[plan.used : plan.used + 1, 0:rows]
                    + line[plan.used : plan.used + 1, rows : 2 * rows]
                )
                rate_out[step : step + 1, :] = rate_row

                @pl.when(block >= plan.group - plan.tail)
                def _():
                    halo[block - (plan.group - plan.tail)] = kv[step][...]

            live = start < info_ref[2] if number == 0 else start + rows > info_ref[2]

            @pl.when(live)
            def _():
                row = rate_row if first_call else rate_ref[step : step + 1, :]
                place = start + lax.broadcasted_iota(jnp.int32, (1, rows), 1)
                member = place < info_ref[2] if number == 0 else place >= info_ref[2]
                rate = column(jnp.where(member, -row, 0.0))
                keys = kv[step][:, 0:width]
                values = kv[step][:, width : 2 * width].astype(F32)
                errors = (rate * values).astype(BF16)
                pre = dot(keys, both_ref[...], 1, 1)
                gate, up = pre[:, 0:width], pre[:, pad : pad + width]
                sigma = jax.nn.sigmoid(gate)
                active = gate * sigma
                hidden = (active * up).astype(BF16)
                back = dot(errors, down_ref[...], 1, 0)
                slope = (back * up * sigma * (1.0 + gate * (1.0 - sigma))).astype(BF16)
                acc_down[...] += dot(errors, hidden, 0, 0)
                acc_both[0:width, :] += dot(slope, keys, 0, 0)
                acc_both[pad : pad + width, :] += dot((back * active).astype(BF16), keys, 0, 0)

        lines[...] = jnp.zeros_like(lines)
        for owner in range(plan.count):
            for kind in range(3):
                for side in range(plan.fold):
                    begin = owner * plan.cols + side * plan.part
                    if kind < 2:
                        piece = acc_both[kind * pad + begin : kind * pad + begin + plan.part, :]
                    else:
                        piece = acc_down[begin : begin + plan.part, :]
                    lines[
                        owner,
                        kind * plan.part : (kind + 1) * plan.part,
                        side * width : (side + 1) * width,
                    ] = piece
        out[...] = lines[...].astype(BF16)

    outputs = (
        jax.ShapeDtypeStruct(plan.wire, BF16),
        jax.ShapeDtypeStruct((2 * pad, width), BF16),
        jax.ShapeDtypeStruct((width, width), BF16),
    )
    if first_call:
        outputs += (
            jax.ShapeDtypeStruct((plan.tail, rows, 2 * width), BF16),
            jax.ShapeDtypeStruct((plan.group, rows), F32),
        )
    return call(
        body,
        info,
        (wire, rates, *blocks),
        outputs,
        [
            pltpu.VMEM((3 * pad, width), F32),
            pltpu.VMEM((2 * pad, width), F32),
            pltpu.VMEM((width, width), F32),
            pltpu.VMEM(plan.wire, F32),
        ],
        flops=12 * plan.group * rows * width * width,
    )


def mixes(plan, info, both, down, queries, number, before=None):
    width, pad, rows = plan.width, plan.pad, plan.rows

    def body(info_ref, both_ref, down_ref, *rest):
        asks, rest = rest[: plan.group], rest[plan.group :]
        olds, outs = (rest[: plan.group], rest[plan.group :]) if number else (None, rest)
        for step in range(plan.group):
            start = block_start(plan, info_ref, step)
            live = start < info_ref[2] if number == 0 else start + rows > info_ref[2]

            @pl.when(live)
            def _():
                pre = dot(unfold(plan, asks[step]), both_ref[...], 1, 1)
                gate, up = pre[:, 0:width], pre[:, pad : pad + width]
                hidden = (gate * jax.nn.sigmoid(gate) * up).astype(BF16)
                mixed = dot(hidden, down_ref[...], 1, 1)
                if number:
                    place = start + lax.broadcasted_iota(jnp.int32, (rows, 1), 0)
                    mixed = jnp.where(
                        place >= info_ref[2], mixed, unfold(plan, olds[step]).astype(F32)
                    )
                fold_into(plan, outs[step], mixed.astype(BF16))

            @pl.when(jnp.logical_not(live))
            def _():
                outs[step][...] = olds[step][...] if number else jnp.zeros_like(outs[step])

    block = jax.ShapeDtypeStruct((plan.half, 2 * width), BF16)
    inputs = (both, down, *queries) + (tuple(before) if number else ())
    return call(
        body,
        info,
        inputs,
        (block,) * plan.group,
        flops=6 * plan.group * rows * width * width,
    )


def attention(plan, info, queries, blocks, halo):
    width, rows, half = plan.width, plan.rows, plan.half
    seen = (plan.tail + 1) * rows
    scale = 1.0 / math.sqrt(width)

    def body(info_ref, halo_ref, *rest):
        asks, rest = rest[: plan.group], rest[plan.group :]
        kv, rest = rest[: plan.group], rest[plan.group :]
        outs, held = rest[: plan.group], rest[plan.group]
        held[0 : plan.tail] = halo_ref[...]
        for step in range(plan.group):
            held[plan.tail + (info_ref[0] ^ step)] = kv[step][...]
        for step in range(plan.group):
            start = block_start(plan, info_ref, step)
            window = held[pl.ds(info_ref[0] ^ step, plan.tail + 1)].reshape(seen, 2 * width)
            line = asks[step][half : half + 16, :].astype(F32)[0:1, :]
            reach = column(line[:, 0:rows] * 16.0 + line[:, rows : 2 * rows]).astype(jnp.int32)
            place = start + lax.broadcasted_iota(jnp.int32, (rows, 1), 0)
            spot = start - plan.tail * rows + lax.broadcasted_iota(jnp.int32, (1, seen), 1)
            allowed = (spot <= place) & (spot >= jnp.maximum(place - reach, 0))
            scores = dot(unfold(plan, asks[step]), window[:, 0:width], 1, 1) * scale
            scores = jnp.where(allowed, scores, -jnp.inf)
            weights = jnp.exp(scores - jnp.max(scores, axis=1, keepdims=True))
            probs = (weights / jnp.sum(weights, axis=1, keepdims=True)).astype(BF16)
            mixed = dot(probs, window[:, width : 2 * width], 1, 0)
            fold_into(plan, outs[step], mixed.astype(BF16))

    block = jax.ShapeDtypeStruct((half, 2 * width), BF16)
    return call(
        body,
        info,
        (halo, *queries, *blocks),
        (block,) * plan.group,
        [pltpu.VMEM((plan.tail + plan.group, rows, 2 * width), BF16)],
        flops=4 * plan.group * rows * seen * width,
    )


def halo_of(plan, last):
    span = plan.group * plan.rows
    shifts = -(-WINDOW // span)
    if shifts == 1:
        pairs = [(i, i + plan.group) for i in range(plan.count - plan.group)]
        return lax.ppermute(last, "tok", pairs)
    parts = []
    for distance in range(shifts, 0, -1):
        hop = distance * plan.group
        parts.append(lax.ppermute(last, "tok", [(i, i + hop) for i in range(plan.count - hop)]))
    return jnp.concatenate(parts, axis=0)[-plan.tail :]


def finish(plan, info, mixed, attended, gain):
    width, half, total = plan.width, plan.half, plan.heads * plan.width

    def body(info_ref, gain_ref, *rest):
        ys, rest = rest[: plan.group], rest[plan.group :]
        adds, out = rest[: plan.group], rest[plan.group]
        squares = [jnp.zeros((half, 1), F32) for _ in range(2)]
        for step in range(plan.group):
            for side in range(2):
                y = ys[step][:, side * width : (side + 1) * width].astype(F32)
                squares[side] += jnp.sum(y * y, axis=1, keepdims=True)
        norms = [lax.rsqrt(s * (1.0 / total) + 1e-06) for s in squares]
        for pair in range(plan.group // 2):
            lanes = pl.ds(pl.multiple_of(((info_ref[0] >> 1) ^ pair) * 2 * width, 128), 2 * width)
            scale = gain_ref[:, lanes]
            for odd in (0, 1):

                @pl.when((info_ref[0] & 1) == odd)
                def _():
                    for side in range(2):
                        own = slice(side * width, (side + 1) * width)
                        steps = (2 * pair + odd, 2 * pair + 1 - odd)
                        y = jnp.concatenate([ys[s][:, own].astype(F32) for s in steps], axis=1)
                        a = jnp.concatenate([adds[s][:, own].astype(F32) for s in steps], axis=1)
                        value = y * norms[side] * scale + a
                        out[side * half : (side + 1) * half, lanes] = value.astype(BF16)

    block = jax.ShapeDtypeStruct((plan.rows, total), BF16)
    return call(body, info, (gain.reshape(1, total), *mixed, *attended), (block,))[0]


def finish_apart(plan, mixed, attended, gain):
    def flat(block):
        return jnp.concatenate([block[:, : plan.width], block[:, plan.width :]], axis=0).astype(F32)

    y, a = flat(mixed[0]), flat(attended[0])
    squares = lax.psum(jnp.sum(y * y, axis=1, keepdims=True), "head")
    mean = squares / (plan.heads * plan.width * lax.axis_size("head"))
    return (y / jnp.sqrt(mean + 1e-06) * gain.reshape(1, -1) + a).astype(BF16)


def spread(wire):
    return lax.all_to_all(wire, "tok", 0, 0, tiled=True)


def on_device(queries, keys, values, rates, back, group_end, gate_init, up_init, down_init, gain):
    rows, heads = rates.shape
    count = lax.axis_size("tok")
    plan = Plan(rows, heads, queries.shape[1] // heads, gate_init.shape[2], count)
    me = lax.axis_index("tok").astype(jnp.int32)
    place = lax.rem(me, plan.group)
    info = jnp.stack([place, (me - place) * rows, group_end[0], me - place])
    states = tuple(jnp.transpose(w, (2, 0, 1)) for w in (gate_init, up_init, down_init))
    rate_rows = rates.T
    reach = back.astype(F32).reshape(1, rows)

    wire = spread(pack_state(plan, info, states, rate_rows))
    blocks = exchange(plan, pack_pair(plan, info, keys, values, "kv"))
    asks = exchange(plan, pack_queries(plan, info, queries, reach))

    found = gradients(plan, info, wire, blocks, rate_rows, 0)
    wire, both, down = found[:3]
    if plan.group > 1:
        last, rate_rows = found[3:]
    else:
        last = blocks[0].reshape(1, rows, -1)
    wire = spread(wire)
    halo = halo_of(plan, last)
    mixed = mixes(plan, info, both, down, asks, 0)
    attended = exchange(plan, attention(plan, info, asks, blocks, halo))
    *states, wire = update(plan, info, states, wire, True)
    wire = spread(wire)
    wire, both, down = gradients(plan, info, wire, blocks, rate_rows, 1)
    wire = spread(wire)
    mixed = exchange(plan, mixes(plan, info, both, down, asks, 1, mixed))
    states = update(plan, info, states, wire, False)
    if plan.group > 1:
        output = finish(plan, info, mixed, attended, gain)
    else:
        output = finish_apart(plan, mixed, attended, gain)
    return (output, *(jnp.transpose(w, (1, 2, 0)) for w in states))


def solution(mesh):
    tokens, state = P("tok", "head"), P("head", None, "tok")
    return jax.shard_map(
        on_device,
        mesh=mesh,
        in_specs=(tokens, tokens, tokens, tokens, P("tok"), P(), state, state, state, P("head")),
        out_specs=(tokens, state, state, state),
        check_vma=False,
    )
```

```python
import functools
import math

import jax
import jax.numpy as jnp
from jax import lax
from jax.experimental import pallas as pl
from jax.experimental.pallas import tpu as pltpu
from jax.sharding import PartitionSpec as P

WINDOW = 512
BF16 = jnp.bfloat16
F32 = jnp.float32
MIB = 1 << 20
MICROSECOND = 10**9
ATT, MIX, GRAD, FINISH, SQUARES, PACK = 10, 8, 12, 10, 30, 30

VMEM = pl.BlockSpec(memory_space=pltpu.VMEM)
SMEM = pl.BlockSpec(memory_space=pltpu.SMEM)
HBM = pl.BlockSpec(memory_space=pltpu.HBM)


def dot(lhs, rhs, lhs_dim, rhs_dim):
    return lax.dot_general(
        lhs, rhs, (((lhs_dim,), (rhs_dim,)), ((), ())), preferred_element_type=F32
    )


def call(
    body, info, inputs, outputs, scratch=(), flops=0, limit=60, late=(), far=(), after=()
):
    moved = sum(math.prod(x.shape) * x.dtype.itemsize for x in [*inputs, *late, *outputs, *far])
    given = 1 + len(inputs) + len(late)

    def kernel(*refs):
        body(*refs[:given], *refs[given + len(after) :])

    return pl.pallas_call(
        kernel,
        out_shape=(*outputs, *far),
        in_specs=[SMEM] + [VMEM] * len(inputs) + [HBM] * (len(late) + len(after)),
        out_specs=(*(VMEM for _ in outputs), *(HBM for _ in far)),
        scratch_shapes=list(scratch),
        compiler_params=pltpu.CompilerParams(vmem_limit_bytes=limit * MIB),
        cost_estimate=pl.CostEstimate(flops=flops, bytes_accessed=0, transcendentals=0),
    )(info, *inputs, *late, *after)


def fetches(sources, targets, semaphores):
    copies = [
        pltpu.make_async_copy(source, target, semaphores.at[number])
        for number, (source, target) in enumerate(zip(sources, targets))
    ]
    for copy in copies:
        copy.start()
    return copies


class Plan:
    def __init__(self, rows, heads, width, cols, count):
        self.rows, self.heads, self.width, self.cols, self.count = rows, heads, width, cols, count
        self.group = heads
        self.planes = count // heads
        self.fold = 2 if cols % 2 == 0 else 1
        self.part = cols // self.fold
        self.used = 3 * self.part
        self.lines = -(-(self.used + 1) // 16) * 16
        self.wide = self.fold * width
        self.pad = -(-width // 128) * 128
        self.gap = self.pad - width
        self.lanes = (slice(0, self.pad), slice(2 * width - self.pad, 2 * width))
        self.half = rows // 2
        self.early = (0, 1, 6, 7) if self.group == 8 else tuple(range(self.group))
        self.late = (2, 3, 4, 5) if self.group == 8 else ()
        self.run = 2 if self.group % 2 == 0 else 1
        self.tail = -(-WINDOW // rows)
        self.wire = (count, self.lines, self.wide)


def pack_state(plan, info, states, rates, after):
    def body(info_ref, gate_in, up_in, down_in, rate_in, out, lines, gate, up, down, rate, sems):
        copies = fetches((gate_in, up_in, down_in, rate_in), (gate, up, down, rate), sems)
        lines[...] = jnp.zeros_like(lines)
        for copy in copies:
            copy.wait()
        for kind, ref in enumerate((gate, up, down)):
            for col in range(plan.cols):
                side, line = divmod(col, plan.part)
                lanes = slice(side * plan.width, (side + 1) * plan.width)
                lines[:, kind * plan.part + line, lanes] = ref[col]
        if plan.group > 1:
            high = rate[...].astype(BF16).astype(F32)
            lines[:, plan.used, 0 : plan.rows] = high
            lines[:, plan.used, plan.rows : 2 * plan.rows] = rate[...] - high
        packed = lines[...].astype(BF16)
        for plane in range(plan.planes):
            out[plane * plan.group : (plane + 1) * plan.group] = packed

    return call(
        body,
        info,
        (),
        (jax.ShapeDtypeStruct(plan.wire, BF16),),
        [pltpu.VMEM((plan.group, plan.lines, plan.wide), F32)]
        + [pltpu.VMEM((plan.cols, plan.heads, plan.width), F32)] * 3
        + [pltpu.VMEM((plan.heads, plan.rows), F32), pltpu.SemaphoreType.DMA((4,))],
        late=(*states, rates),
        after=after,
    )[0]


def update(plan, info, states, wire, send, after=()):
    def body(info_ref, wire_ref, gate_in, up_in, down_in, *rest):
        if not send:
            rest = (*rest[:-1], gate_in, up_in, down_in, None)
        news, rest = rest[:3], rest[3:]
        out = rest[0] if send else None
        total, grad, gate, up, down, sems = rest[-6:]
        copies = fetches((gate_in, up_in, down_in), (gate, up, down), sems) if send else ()
        acc = wire_ref[0 : plan.group].astype(F32)
        for plane in range(1, plan.planes):
            acc += wire_ref[plane * plan.group : (plane + 1) * plan.group].astype(F32)
        total[...] = acc
        for kind, ref in enumerate((gate, up, down)):
            for col in range(plan.cols):
                side, line = divmod(col, plan.part)
                lanes = slice(side * plan.width, (side + 1) * plan.width)
                grad[col] = total[:, kind * plan.part + line, lanes]
            if send:
                copies[kind].wait()
            old = ref[...]
            fresh = old - grad[...]
            old_norm = jnp.sqrt(jnp.sum(old * old, axis=2, keepdims=True))
            new_norm = jnp.sqrt(jnp.sum(fresh * fresh, axis=2, keepdims=True) + 1e-06)
            new = fresh * (old_norm / new_norm)
            news[kind][...] = new
            if send:
                for col in range(plan.cols):
                    side, line = divmod(col, plan.part)
                    lanes = slice(side * plan.width, (side + 1) * plan.width)
                    total[:, kind * plan.part + line, lanes] = new[col]
        if send:
            packed = total[...].astype(BF16)
            for plane in range(plan.planes):
                out[plane * plan.group : (plane + 1) * plan.group] = packed

    state = jax.ShapeDtypeStruct((plan.cols, plan.heads, plan.width), F32)
    outputs = (state, state, state)
    if send:
        outputs += (jax.ShapeDtypeStruct(plan.wire, BF16),)
    return call(
        body,
        info,
        (wire,) if send else (wire, *states),
        outputs,
        [pltpu.VMEM((plan.group, plan.lines, plan.wide), F32)]
        + [pltpu.VMEM((plan.cols, plan.heads, plan.width), F32)] * (4 if send else 1)
        + [pltpu.SemaphoreType.DMA((3,))],
        late=states if send else (),
        after=after,
    )


def pack_pair(plan, info, left, right):
    def body(info_ref, left_in, right_in, *rest):
        outs, (left_ref, right_ref, held, sems, sent) = rest[: plan.group], rest[plan.group :]
        copies = []
        for copy in fetches((left_in, right_in), (left_ref, right_ref), sems):
            copy.wait()
        for step in range(plan.group):
            head = info_ref[0] ^ step
            lanes = pl.ds(pl.multiple_of((head >> 1) * 2 * plan.width, 128), 2 * plan.width)
            for odd in (0, 1):

                @pl.when((head & 1) == odd)
                def _():
                    own = slice(odd * plan.width, (odd + 1) * plan.width)
                    held[step, :, 0 : plan.width] = left_ref[:, lanes][:, own]
                    held[step, :, plan.width : 2 * plan.width] = right_ref[:, lanes][:, own]

            copies += fetches([held.at[step]], [outs[step]], sent.at[pl.ds(step, 1)])
        for copy in copies:
            copy.wait()

    if plan.group == 1:
        return (jnp.concatenate([left, right], axis=1),)
    block = jax.ShapeDtypeStruct((plan.rows, 2 * plan.width), BF16)
    return call(
        body,
        info,
        (),
        (),
        [pltpu.VMEM(left.shape, BF16)] * 2
        + [
            pltpu.VMEM((plan.group, plan.rows, 2 * plan.width), BF16),
            pltpu.SemaphoreType.DMA((2,)),
            pltpu.SemaphoreType.DMA((plan.group,)),
        ],
        late=(left, right),
        far=(block,) * plan.group,
    )


def last_blocks(plan, info, blocks, after=()):
    def body(info_ref, *refs):
        sources, (out, held, sems, sent) = refs[: plan.group], refs[plan.group :]

        def each(act):
            for step in range(plan.group):
                block = (info_ref[0] ^ step) - (plan.group - plan.tail)

                @pl.when(block >= 0)
                def _():
                    act(pltpu.make_async_copy(sources[step], held.at[block], sems.at[step]))

        each(lambda copy: copy.start())
        each(lambda copy: copy.wait())
        fetches([held], [out], sent)[0].wait()

    if plan.group == 1:
        return blocks[0].reshape(1, plan.rows, -1)
    block = jax.ShapeDtypeStruct((plan.tail, plan.rows, 2 * plan.width), BF16)
    scratch = [pltpu.VMEM(block.shape, BF16)]
    scratch += [pltpu.SemaphoreType.DMA((size,)) for size in (plan.group, 1)]
    return call(body, info, (), (), scratch, late=blocks, far=(block,), after=after)[0]


def pack_queries(plan, info, queries, reach, steps, after=()):
    half, width = plan.half, plan.width

    def fill(out, own, line):
        out[0:half, 0:width] = own[0:half]
        out[0:half, width : 2 * width] = own[half : 2 * half]
        out[half : half + 16, 0 : 2 * plan.rows] = line
        out[half : half + 16, 2 * plan.rows :] = jnp.zeros((16, 2 * (width - plan.rows)), BF16)

    def body(info_ref, back_ref, query_in, *rest):
        outs, (query_ref, held, sems, sent) = rest[: len(steps)], rest[len(steps) :]
        copies = fetches([query_in], [query_ref], sems)
        back = back_ref[...]
        high = jnp.floor(back * (1.0 / 16.0))
        line = jnp.concatenate([high, back - 16.0 * high], axis=1)
        line = (jnp.zeros((16, 2 * plan.rows), F32) + line).astype(BF16)
        copies.pop().wait()
        for number, step in enumerate(steps):
            if plan.group == 1:
                fill(held.at[0], query_ref[...], line)
            head = info_ref[0] ^ step
            lanes = pl.ds(pl.multiple_of((head >> 1) * 2 * width, 128), 2 * width)
            for odd in (0, 1) if plan.group > 1 else ():

                @pl.when((head & 1) == odd)
                def _():
                    own = slice(odd * width, (odd + 1) * width)
                    fill(held.at[number], query_ref[:, lanes][:, own], line)

            copies += fetches([held.at[number]], [outs[number]], sent.at[pl.ds(number, 1)])
        for copy in copies:
            copy.wait()

    block = jax.ShapeDtypeStruct((half + 16, 2 * width), BF16)
    return call(
        body,
        info,
        (reach,),
        (),
        [
            pltpu.VMEM(queries.shape, BF16),
            pltpu.VMEM((len(steps), half + 16, 2 * width), BF16),
            pltpu.SemaphoreType.DMA((1,)),
            pltpu.SemaphoreType.DMA((len(steps),)),
        ],
        late=(queries,),
        far=(block,) * len(steps),
        flops=PACK * MICROSECOND,
        after=after,
    )


def exchange(plan, blocks, steps=None):
    moved = {}
    for step in range(plan.group) if steps is None else steps:
        pairs = [(source, source ^ step) for source in range(plan.count)]
        moved[step] = lax.ppermute(blocks[step], "tok", pairs) if step else blocks[0]
    return moved


def sigmoid(value):
    return 0.5 * jnp.tanh(0.5 * value) + 0.5


def column(row):
    return jnp.swapaxes(jnp.broadcast_to(row, (8, row.shape[1])), 0, 1)[:, 0:1]


def line_places(plan):
    for owner in range(plan.count):
        for kind in range(3):
            for side in range(plan.fold):
                lines = slice(kind * plan.part, (kind + 1) * plan.part)
                lanes = slice(side * plan.width, (side + 1) * plan.width)
                yield owner, kind, lines, lanes, owner * plan.cols + side * plan.part


def fill_wire(plan, acc_both, acc_down, out, turned, lines):
    turned[0 : plan.pad] = acc_both[:, 0 : plan.pad].T
    turned[plan.pad : 2 * plan.pad] = acc_both[:, plan.pad :].T
    lines[:, plan.used :, :] = jnp.zeros((plan.count, plan.lines - plan.used, plan.wide), F32)
    for owner, kind, where, lanes, begin in line_places(plan):
        if kind < 2:
            piece = turned[kind * plan.pad + begin : kind * plan.pad + begin + plan.part, :]
        else:
            piece = acc_down[plan.gap + begin : plan.gap + begin + plan.part, :]
        lines[owner, where, lanes] = piece[:, 0 : plan.width]
    out[...] = lines[...].astype(BF16)


def unpack(plan, wire_ref, wide, both_ref, down_ref):
    width, pad, gap = plan.width, plan.pad, plan.gap
    if gap:
        wide[:, :, width:] = jnp.zeros((3, pad, gap), F32)
        wide[0:2, width:, :] = jnp.zeros((2, gap, pad), F32)
        wide[2, 0:gap, :] = jnp.zeros((gap, pad), F32)
    chunk = None
    for owner, kind, where, lanes, begin in line_places(plan):
        if kind == 0 and lanes.start == 0:
            chunk = wire_ref[owner].astype(F32)
        begin += gap if kind == 2 else 0
        wide[kind, begin : begin + plan.part, 0:width] = chunk[where, lanes]
    both_ref[:, 0:pad] = wide[0].T.astype(BF16)
    both_ref[:, pad:] = wide[1].T.astype(BF16)
    down_ref[...] = wide[2].astype(BF16)


def weights_of(plan, info, wire, after=()):
    rows = plan.rows

    def body(info_ref, wire_ref, both_ref, down_ref, rate_out, wide):
        unpack(plan, wire_ref, wide, both_ref, down_ref)
        for block in range(plan.group if plan.group > 1 else 0):
            line = wire_ref[info_ref[3] + block].astype(F32)[plan.used : plan.used + 1]
            rate_out[block : block + 1, :] = line[:, 0:rows] + line[:, rows : 2 * rows]

    pad = plan.pad
    return call(
        body,
        info,
        (wire,),
        (
            jax.ShapeDtypeStruct((pad, 2 * pad), BF16),
            jax.ShapeDtypeStruct((pad, pad), BF16),
            jax.ShapeDtypeStruct((plan.group, rows), F32),
        ),
        [pltpu.VMEM((3, pad, pad), F32)],
        after=after,
    )


def gradients(plan, info, weights, blocks, rates, number, after=()):
    width, pad, rows = plan.width, plan.pad, plan.rows
    wired = len(weights) == 1

    def body(info_ref, rate_ref, *rest):
        weight_refs, rest = rest[: len(weights)], rest[len(weights) :]
        sources, rest = rest[: plan.group], rest[plan.group :]
        out, rest = rest[0], rest[1:]
        if wired:
            weight_refs, wire_ref, rest = rest[:2], weight_refs[0], rest[2:]
        both_ref, down_ref = weight_refs
        kv, sems, acc_both, acc_down, turned, lines, *wide = rest
        targets = [kv.at[info_ref[0] ^ step] for step in range(plan.group)]
        copies = fetches(sources, targets, sems)
        if wired:
            unpack(plan, wire_ref, wide[0], both_ref, down_ref)
        acc_both[...] = jnp.zeros_like(acc_both)
        acc_down[...] = jnp.zeros_like(acc_down)
        for copy in copies:
            copy.wait()
        for run in range(0, plan.group, plan.run):
            start = info_ref[1] + run * rows
            live = start < info_ref[2] if number == 0 else start + plan.run * rows > info_ref[2]

            @pl.when(live)
            def _():
                for block in range(run, run + plan.run):
                    place = info_ref[1] + block * rows
                    place += lax.broadcasted_iota(jnp.int32, (1, rows), 1)
                    member = place < info_ref[2] if number == 0 else place >= info_ref[2]
                    rate = column(jnp.where(member, -rate_ref[block : block + 1, :], 0.0))
                    keys = kv[block, :, plan.lanes[0]]
                    errors = (rate * kv[block, :, plan.lanes[1]].astype(F32)).astype(BF16)
                    pre = dot(keys, both_ref[...], 1, 0)
                    back = dot(errors, down_ref[...], 1, 0)
                    gate, up = pre[:, 0:pad], pre[:, pad:]
                    sigma = sigmoid(gate)
                    active = gate * sigma
                    hidden = (active * up).astype(BF16)
                    turn = sigma + active * (1.0 - sigma)
                    slope = (back * up * turn).astype(BF16)
                    joint = jnp.concatenate([slope, (back * active).astype(BF16)], axis=1)
                    acc_both[...] += dot(keys, joint, 0, 0)
                    acc_down[...] += dot(errors, hidden, 0, 0)

        fill_wire(plan, acc_both, acc_down, out, turned, lines)

    outputs = (jax.ShapeDtypeStruct(plan.wire, BF16),)
    if wired:
        outputs += (
            jax.ShapeDtypeStruct((pad, 2 * pad), BF16),
            jax.ShapeDtypeStruct((pad, pad), BF16),
        )
    scratch = [
        pltpu.VMEM((plan.group, rows, 2 * width), BF16),
        pltpu.SemaphoreType.DMA((plan.group,)),
        pltpu.VMEM((pad, 2 * pad), F32),
        pltpu.VMEM((pad, pad), F32),
        pltpu.VMEM((2 * pad, pad), F32),
        pltpu.VMEM(plan.wire, F32),
    ]
    if wired:
        scratch.append(pltpu.VMEM((3, pad, pad), F32))
    return call(
        body,
        info,
        (rates, *weights),
        outputs,
        scratch,
        flops=GRAD * MICROSECOND,
        late=blocks,
        after=after,
    )


def unfold(plan, ref):
    half, width = plan.half, plan.width
    first = ref[0:half, plan.lanes[0]]
    second = ref[0:half, plan.lanes[1]]
    second = jnp.concatenate([second[:, plan.gap :], second[:, 0 : plan.gap]], axis=1)
    lane = lax.broadcasted_iota(jnp.int32, (1, plan.pad), 1)
    keep = jnp.where(lane < width, 1.0, 0.0).astype(BF16)
    return jnp.concatenate([first, second], axis=0) * keep


def fold(plan, value):
    half, gap, pad = plan.half, plan.gap, plan.pad
    return jnp.concatenate([value[0:half, gap:], value[half:, gap:]], axis=1)


def mixes(plan, info, steps, both, down, queries, number, before=(), after=()):
    count = len(steps)
    width, pad, rows, half = plan.width, plan.pad, plan.rows, plan.half

    def body(info_ref, both_ref, down_ref, *rest):
        sources, rest = rest[:count], rest[count:]
        old_in, rest = (rest[:count], rest[count:]) if number else ((), rest)
        outs, rest = rest[:count], rest[count:]
        asks, olds, news, turned, sems, sent = rest
        place = info_ref[0]
        targets = [held.at[index] for held in (asks, olds) for index in range(count)]
        copies = fetches((*sources, *old_in), targets, sems)
        turned[...] = down_ref[...].astype(F32).T.astype(BF16)
        for copy in copies:
            copy.wait()
        for index in range(0, count, plan.run):
            both_of = range(index, index + plan.run)
            starts = [info_ref[1] + (place ^ steps[i]) * rows for i in both_of]
            start = functools.reduce(jnp.minimum, starts)
            live = start < info_ref[2] if number == 0 else start + plan.run * rows > info_ref[2]

            @pl.when(live)
            def _():
                asked = jnp.concatenate([unfold(plan, asks.at[i]) for i in both_of], axis=0)
                pre = dot(asked, both_ref[...], 1, 0)
                gate, up = pre[:, 0:pad], pre[:, pad:]
                hidden = (gate * sigmoid(gate) * up).astype(BF16)
                result = dot(hidden, turned[...], 1, 0)
                for at, i in enumerate(both_of):
                    new = fold(plan, result[at * rows : (at + 1) * rows])
                    if number:
                        spot = starts[at] + lax.broadcasted_iota(jnp.int32, new.shape, 0)
                        lane = lax.broadcasted_iota(jnp.int32, new.shape, 1)
                        spot += jnp.where(lane >= width, half, 0)
                        new = jnp.where(spot >= info_ref[2], new, olds[i].astype(F32))
                    news[i] = new.astype(BF16)

            @pl.when(jnp.logical_not(live))
            def _():
                for i in both_of:
                    news[i] = olds[i] if number else jnp.zeros_like(olds[i])

        for copy in fetches([news.at[index] for index in range(count)], outs, sent):
            copy.wait()

    block = jax.ShapeDtypeStruct((half, 2 * width), BF16)
    return call(
        body,
        info,
        (both, down),
        (),
        [
            pltpu.VMEM((count, half + 16, 2 * width), BF16),
            pltpu.VMEM((count, half, 2 * width), BF16),
            pltpu.VMEM((count, half, 2 * width), BF16),
            pltpu.VMEM((pad, pad), BF16),
            pltpu.SemaphoreType.DMA((2 * count,)),
            pltpu.SemaphoreType.DMA((count,)),
        ],
        far=(block,) * count,
        flops=MIX * MICROSECOND,
        late=(*queries, *before),
        after=after,
    )


def attention(plan, info, steps, queries, blocks, halo, after=()):
    count = len(steps)
    width, pad, rows, half = plan.width, plan.pad, plan.rows, plan.half
    seen = (plan.tail + 1) * rows
    scale = 1.0 / math.sqrt(width)

    def body(info_ref, halo_in, *rest):
        sources, rest = rest[: count + plan.group], rest[count + plan.group :]
        outs, rest = rest[:count], rest[count:]
        asks, held, news, sems, sent = rest
        place = info_ref[0]
        targets = [held.at[0 : plan.tail]]
        targets += [asks.at[number] for number in range(count)]
        targets += [held.at[plan.tail + (place ^ step)] for step in range(plan.group)]
        for copy in fetches((halo_in, *sources), targets, sems):
            copy.wait()
        query = lax.broadcasted_iota(jnp.int32, (rows, 1), 0) + plan.tail * rows
        spot = lax.broadcasted_iota(jnp.int32, (rows, seen), 1)
        for number, step in enumerate(steps):
            block = place ^ step
            line = asks[number, half : half + 16, :].astype(F32)[0:1, :]
            reach = column(line[:, 0:rows] * 16.0 + line[:, rows : 2 * rows]).astype(jnp.int32)
            first = plan.tail * rows - info_ref[1] - block * rows
            low = jnp.maximum(query - reach, first)
            window = held[pl.ds(block, plan.tail + 1)].reshape(seen, 2 * width)
            scores = dot(unfold(plan, asks.at[number]), window[:, plan.lanes[0]], 1, 1)
            scores = jnp.where((spot <= query) & (spot >= low), scores, -jnp.inf)
            top = jnp.max(scores, axis=1, keepdims=True)
            weights = jnp.exp((scores - top) * scale)
            total = jnp.sum(weights, axis=1, keepdims=True)
            mixed = dot(weights.astype(BF16), window[:, plan.lanes[1]], 1, 0)
            news[number] = fold(plan, mixed * (1.0 / total)).astype(BF16)
        for copy in fetches([news.at[number] for number in range(count)], outs, sent):
            copy.wait()

    block = jax.ShapeDtypeStruct((half, 2 * width), BF16)
    return call(
        body,
        info,
        (),
        (),
        [
            pltpu.VMEM((count, half + 16, 2 * width), BF16),
            pltpu.VMEM((plan.tail + plan.group, rows, 2 * width), BF16),
            pltpu.VMEM((count, half, 2 * width), BF16),
            pltpu.SemaphoreType.DMA((1 + count + plan.group,)),
            pltpu.SemaphoreType.DMA((count,)),
        ],
        far=(block,) * count,
        flops=ATT * MICROSECOND,
        late=(halo, *queries, *blocks),
        after=after,
    )


def halo_of(plan, last):
    span = plan.group * plan.rows
    shifts = -(-WINDOW // span)
    if shifts == 1:
        pairs = [(i, i + plan.group) for i in range(plan.count - plan.group)]
        return lax.ppermute(last, "tok", pairs)
    parts = []
    for distance in range(shifts, 0, -1):
        hop = distance * plan.group
        parts.append(lax.ppermute(last, "tok", [(i, i + hop) for i in range(plan.count - hop)]))
    return jnp.concatenate(parts, axis=0)[-plan.tail :]


def squares_of(plan, info, blocks):
    def body(info_ref, *refs):
        count = len(blocks)
        out, held, sems = refs[count:]
        total = jnp.zeros(out.shape, F32)
        places = [held.at[index] for index in range(count)]
        for index, copy in enumerate(fetches(refs[:count], places, sems)):
            copy.wait()
            y = held[index].astype(F32)
            total += y * y
        out[...] = total

    shape = (plan.half, 2 * plan.width)
    return call(
        body,
        info,
        (),
        (jax.ShapeDtypeStruct(shape, F32),),
        [pltpu.VMEM((len(blocks), *shape), BF16), pltpu.SemaphoreType.DMA((len(blocks),))],
        flops=SQUARES * MICROSECOND,
        late=blocks,
    )[0]


def finish(plan, info, mixed, attended, gain, squares, after):
    width, half, total = plan.width, plan.half, plan.heads * plan.width

    def body(info_ref, gain_ref, squares_ref, *rest):
        sources, rest = rest[: 2 * plan.group], rest[2 * plan.group :]
        out_far, ys, adds, out, sems, sent = rest
        targets = [held.at[step] for held in (ys, adds) for step in range(plan.group)]
        copies = fetches(sources, targets, sems)
        done = []
        squares = squares_ref[...]
        for step in range(plan.group):
            copies[step].wait()
            if step in plan.early:
                continue
            y = ys[step].astype(F32)
            squares += y * y
        norms = [
            lax.rsqrt(jnp.sum(s, axis=1, keepdims=True) * (1.0 / total) + 1e-06)
            for s in (squares[:, 0:width], squares[:, width:])
        ]
        lane = lax.broadcasted_iota(jnp.int32, (half, 2 * width), 1)
        norm = jnp.where(lane < width, norms[0], norms[1])
        for pair in range(plan.group // 2):
            lanes = pl.ds(pl.multiple_of(((info_ref[0] >> 1) ^ pair) * 2 * width, 128), 2 * width)
            values = []
            for step in (2 * pair, 2 * pair + 1):
                copies[plan.group + step].wait()
                scale = gain_ref[pl.ds(info_ref[0] ^ step, 1), :]
                value = ys[step].astype(F32) * norm * scale + adds[step].astype(F32)
                values.append(value.astype(BF16))
            for odd in (0, 1):

                @pl.when((info_ref[0] & 1) == odd)
                def _():
                    even, other = values[odd], values[1 - odd]
                    for side in range(2):
                        own = slice(side * width, (side + 1) * width)
                        joined = jnp.concatenate([even[:, own], other[:, own]], axis=1)
                        out[pair, side * half : (side + 1) * half, :] = joined

            done += fetches([out.at[pair]], [out_far.at[:, lanes]], sent.at[pl.ds(pair, 1)])
        for copy in done:
            copy.wait()

    gain = gain.reshape(plan.heads, width)
    return call(
        body,
        info,
        (jnp.concatenate([gain, gain], axis=1), squares),
        (),
        [
            pltpu.VMEM((plan.group, half, 2 * width), BF16),
            pltpu.VMEM((plan.group, half, 2 * width), BF16),
            pltpu.VMEM((plan.group // 2, plan.rows, 2 * width), BF16),
            pltpu.SemaphoreType.DMA((2 * plan.group,)),
            pltpu.SemaphoreType.DMA((plan.group // 2,)),
        ],
        late=tuple(held[step] for held in (mixed, attended) for step in range(plan.group)),
        far=(jax.ShapeDtypeStruct((plan.rows, total), BF16),),
        flops=FINISH * MICROSECOND,
        after=after,
    )[0]


def finish_apart(plan, mixed, attended, gain):
    def flat(block):
        return jnp.concatenate([block[:, : plan.width], block[:, plan.width :]], axis=0).astype(F32)

    y, a = flat(mixed[0]), flat(attended[0])
    squares = lax.psum(jnp.sum(y * y, axis=1, keepdims=True), "head")
    mean = squares / (plan.heads * plan.width * lax.axis_size("head"))
    return (y / jnp.sqrt(mean + 1e-06) * gain.reshape(1, -1) + a).astype(BF16)


def spread(wire):
    return lax.all_to_all(wire, "tok", 0, 0, tiled=True)


def on_device(queries, keys, values, rates, back, group_end, gate_init, up_init, down_init, gain):
    rows, heads = rates.shape
    count = lax.axis_size("tok")
    plan = Plan(rows, heads, queries.shape[1] // heads, gate_init.shape[2], count)
    me = lax.axis_index("tok").astype(jnp.int32)
    place = lax.rem(me, plan.group)
    info = jnp.stack([place, (me - place) * rows, group_end[0], me - place])
    states = tuple(jnp.transpose(w, (2, 0, 1)) for w in (gate_init, up_init, down_init))
    rate_rows = rates.T
    reach = back.astype(F32).reshape(1, rows)

    packed = pack_pair(plan, info, keys, values)
    blocks = [*exchange(plan, packed).values()]
    wire = spread(pack_state(plan, info, states, rate_rows, packed[:1]))
    both, down, found = weights_of(plan, info, wire)
    if plan.group > 1:
        rate_rows = found

    def part(steps, blocks):
        return [blocks[step] for step in steps]

    early, late = plan.early, plan.late
    steps = (*early, *late)
    last = last_blocks(plan, info, blocks, (down,))
    wire = gradients(plan, info, (both, down), blocks, rate_rows, 0, (last,))[0]
    halo = halo_of(plan, last)
    found = pack_queries(plan, info, queries, reach, steps, (wire, halo))
    asks = exchange(plan, dict(zip(steps, found)))
    wire = spread(wire)
    *states, wire = update(plan, info, states, wire, True, part(early[1:3], asks))
    wire, after = spread(wire), (wire,)
    found = attention(plan, info, steps, part(steps, asks), blocks, halo, after)
    attended, after = dict(zip(steps, found)), found[:1]
    found = mixes(plan, info, steps, both, down, part(steps, asks), 0, after=after)
    before = dict(zip(steps, found))
    attended = exchange(plan, attended)
    both, down, _ = weights_of(plan, info, wire, found[:1])
    found = mixes(plan, info, early, both, down, part(early, asks), 1, part(early, before))
    after = (*found[:1], *part(early[1:], attended))
    wire = gradients(plan, info, (both, down), blocks, rate_rows, 1, after)[0]
    mixed = exchange(plan, dict(zip(early, found)), early)
    if late:
        squares = squares_of(plan, info, part(early, mixed))
        found = mixes(plan, info, late, both, down, part(late, asks), 1, part(late, before), (wire, mixed[1]))
        mixed.update(exchange(plan, dict(zip(late, found)), late))
    wire = spread(wire)
    if not late:
        squares = squares_of(plan, info, part(early, mixed))
    states = update(plan, info, states, wire, False, (squares,))
    if plan.group > 1:
        output = finish(plan, info, mixed, attended, gain, squares, states[:1])
    else:
        output = finish_apart(plan, mixed, attended, gain)
    return (output, *(jnp.transpose(w, (1, 2, 0)) for w in states))


def solution(mesh):
    tokens, state = P("tok", "head"), P("head", None, "tok")
    return jax.shard_map(
        on_device,
        mesh=mesh,
        in_specs=(tokens, tokens, tokens, tokens, P("tok"), P(), state, state, state, P("head")),
        out_specs=(tokens, state, state, state),
        check_vma=False,
    )
```

```python
import functools
import math

import jax
import jax.numpy as jnp
from jax import lax
from jax.experimental import pallas as pl
from jax.experimental.pallas import tpu as pltpu
from jax.sharding import PartitionSpec as P

WINDOW = 512
BF16 = jnp.bfloat16
F32 = jnp.float32
MIB = 1 << 20
MICROSECOND = 10**9
ATT, MIX, GRAD, DELAY, FINISH, PACK = 10, 8, 12, 20, 10, 30
SPENT = 40

VMEM = pl.BlockSpec(memory_space=pltpu.VMEM)
SMEM = pl.BlockSpec(memory_space=pltpu.SMEM)
HBM = pl.BlockSpec(memory_space=pltpu.HBM)


def dot(lhs, rhs, lhs_dim, rhs_dim):
    return lax.dot_general(
        lhs, rhs, (((lhs_dim,), (rhs_dim,)), ((), ())), preferred_element_type=F32
    )


def call(
    body, info, inputs, outputs, scratch=(), flops=0, limit=60, late=(), far=(), after=()
):
    moved = sum(math.prod(x.shape) * x.dtype.itemsize for x in [*inputs, *late, *outputs, *far])
    given = 1 + len(inputs) + len(late)

    def kernel(*refs):
        body(*refs[:given], *refs[given + len(after) :])

    return pl.pallas_call(
        kernel,
        out_shape=(*outputs, *far),
        in_specs=[SMEM] + [VMEM] * len(inputs) + [HBM] * (len(late) + len(after)),
        out_specs=(*(VMEM for _ in outputs), *(HBM for _ in far)),
        scratch_shapes=list(scratch),
        compiler_params=pltpu.CompilerParams(vmem_limit_bytes=limit * MIB),
        cost_estimate=pl.CostEstimate(flops=flops, bytes_accessed=0, transcendentals=0),
    )(info, *inputs, *late, *after)


def fetches(sources, targets, semaphores):
    copies = [
        pltpu.make_async_copy(source, target, semaphores.at[number])
        for number, (source, target) in enumerate(zip(sources, targets))
    ]
    for copy in copies:
        copy.start()
    return copies


class Plan:
    def __init__(self, rows, heads, width, cols, count):
        self.rows, self.heads, self.width, self.cols, self.count = rows, heads, width, cols, count
        self.group = heads
        self.planes = count // heads
        self.fold = 2 if cols % 2 == 0 else 1
        self.part = cols // self.fold
        self.used = 3 * self.part
        self.lines = -(-(self.used + 1) // 16) * 16
        self.wide = self.fold * width
        self.pad = -(-width // 128) * 128
        self.gap = self.pad - width
        self.lanes = (slice(0, self.pad), slice(2 * width - self.pad, 2 * width))
        self.half = rows // 2
        self.steps = tuple(range(self.group))
        self.order = (0, 6, 7, 2, 4, 3, 5, 1) if self.group == 8 else self.steps
        self.run = 2 if self.group % 2 == 0 else 1
        self.tail = -(-WINDOW // rows)
        self.wire = (count, self.lines, self.wide)


def pack_state(plan, info, states, rates, after):
    def body(info_ref, gate_in, up_in, down_in, rate_in, out, lines, gate, up, down, rate, sems):
        copies = fetches((gate_in, up_in, down_in, rate_in), (gate, up, down, rate), sems)
        lines[...] = jnp.zeros_like(lines)
        for copy in copies:
            copy.wait()
        for kind, ref in enumerate((gate, up, down)):
            for col in range(plan.cols):
                side, line = divmod(col, plan.part)
                lanes = slice(side * plan.width, (side + 1) * plan.width)
                lines[:, kind * plan.part + line, lanes] = ref[col]
        if plan.group > 1:
            high = rate[...].astype(BF16).astype(F32)
            lines[:, plan.used, 0 : plan.rows] = high
            lines[:, plan.used, plan.rows : 2 * plan.rows] = rate[...] - high
        packed = lines[...].astype(BF16)
        for plane in range(plan.planes):
            out[plane * plan.group : (plane + 1) * plan.group] = packed

    return call(
        body,
        info,
        (),
        (jax.ShapeDtypeStruct(plan.wire, BF16),),
        [pltpu.VMEM((plan.group, plan.lines, plan.wide), F32)]
        + [pltpu.VMEM((plan.cols, plan.heads, plan.width), F32)] * 3
        + [pltpu.VMEM((plan.heads, plan.rows), F32), pltpu.SemaphoreType.DMA((4,))],
        late=(*states, rates),
        after=after,
    )[0]


def update(plan, info, states, wire, send, after=()):
    def body(info_ref, wire_ref, gate_in, up_in, down_in, *rest):
        if not send:
            rest = (*rest[:-1], gate_in, up_in, down_in, None)
        news, rest = rest[:3], rest[3:]
        out = rest[0] if send else None
        total, grad, gate, up, down, sems = rest[-6:]
        copies = fetches((gate_in, up_in, down_in), (gate, up, down), sems) if send else ()
        acc = wire_ref[0 : plan.group].astype(F32)
        for plane in range(1, plan.planes):
            acc += wire_ref[plane * plan.group : (plane + 1) * plan.group].astype(F32)
        total[...] = acc
        for kind, ref in enumerate((gate, up, down)):
            for col in range(plan.cols):
                side, line = divmod(col, plan.part)
                lanes = slice(side * plan.width, (side + 1) * plan.width)
                grad[col] = total[:, kind * plan.part + line, lanes]
            if send:
                copies[kind].wait()
            old = ref[...]
            fresh = old - grad[...]
            old_norm = jnp.sqrt(jnp.sum(old * old, axis=2, keepdims=True))
            new_norm = jnp.sqrt(jnp.sum(fresh * fresh, axis=2, keepdims=True) + 1e-06)
            new = fresh * (old_norm / new_norm)
            news[kind][...] = new
            if send:
                for col in range(plan.cols):
                    side, line = divmod(col, plan.part)
                    lanes = slice(side * plan.width, (side + 1) * plan.width)
                    total[:, kind * plan.part + line, lanes] = new[col]
        if send:
            packed = total[...].astype(BF16)
            for plane in range(plan.planes):
                out[plane * plan.group : (plane + 1) * plan.group] = packed

    state = jax.ShapeDtypeStruct((plan.cols, plan.heads, plan.width), F32)
    outputs = (state, state, state)
    if send:
        outputs += (jax.ShapeDtypeStruct(plan.wire, BF16),)
    return call(
        body,
        info,
        (wire,) if send else (wire, *states),
        outputs,
        [pltpu.VMEM((plan.group, plan.lines, plan.wide), F32)]
        + [pltpu.VMEM((plan.cols, plan.heads, plan.width), F32)] * (4 if send else 1)
        + [pltpu.SemaphoreType.DMA((3,))],
        late=states if send else (),
        after=after,
    )


def pack_pair(plan, info, left, right):
    def body(info_ref, left_in, right_in, *rest):
        outs, (left_ref, right_ref, held, sems, sent) = rest[: plan.group], rest[plan.group :]
        copies = []
        for copy in fetches((left_in, right_in), (left_ref, right_ref), sems):
            copy.wait()
        for step in range(plan.group):
            head = info_ref[0] ^ plan.order[step]
            lanes = pl.ds(pl.multiple_of((head >> 1) * 2 * plan.width, 128), 2 * plan.width)
            for odd in (0, 1):

                @pl.when((head & 1) == odd)
                def _():
                    own = slice(odd * plan.width, (odd + 1) * plan.width)
                    held[step, :, 0 : plan.width] = left_ref[:, lanes][:, own]
                    held[step, :, plan.width : 2 * plan.width] = right_ref[:, lanes][:, own]

            copies += fetches([held.at[step]], [outs[step]], sent.at[pl.ds(step, 1)])
        for copy in copies:
            copy.wait()

    if plan.group == 1:
        return (jnp.concatenate([left, right], axis=1),)
    block = jax.ShapeDtypeStruct((plan.rows, 2 * plan.width), BF16)
    return call(
        body,
        info,
        (),
        (),
        [pltpu.VMEM(left.shape, BF16)] * 2
        + [
            pltpu.VMEM((plan.group, plan.rows, 2 * plan.width), BF16),
            pltpu.SemaphoreType.DMA((2,)),
            pltpu.SemaphoreType.DMA((plan.group,)),
        ],
        late=(left, right),
        far=(block,) * plan.group,
    )


def last_blocks(plan, info, blocks, after=()):
    def body(info_ref, *refs):
        sources, (out, held, sems, sent) = refs[: plan.group], refs[plan.group :]

        def each(act):
            for step in range(plan.group):
                block = (info_ref[0] ^ plan.order[step]) - (plan.group - plan.tail)

                @pl.when(block >= 0)
                def _():
                    act(pltpu.make_async_copy(sources[step], held.at[block], sems.at[step]))

        each(lambda copy: copy.start())
        each(lambda copy: copy.wait())
        fetches([held], [out], sent)[0].wait()

    if plan.group == 1:
        return blocks[0].reshape(1, plan.rows, -1)
    block = jax.ShapeDtypeStruct((plan.tail, plan.rows, 2 * plan.width), BF16)
    scratch = [pltpu.VMEM(block.shape, BF16)]
    scratch += [pltpu.SemaphoreType.DMA((size,)) for size in (plan.group, 1)]
    return call(body, info, (), (), scratch, late=blocks, far=(block,), after=after)[0]


def pack_queries(plan, info, queries, reach, steps, after=()):
    half, width = plan.half, plan.width

    def fill(out, own, line):
        out[0:half, 0:width] = own[0:half]
        out[0:half, width : 2 * width] = own[half : 2 * half]
        out[half : half + 16, 0 : 2 * plan.rows] = line
        out[half : half + 16, 2 * plan.rows :] = jnp.zeros((16, 2 * (width - plan.rows)), BF16)

    def body(info_ref, back_ref, query_in, *rest):
        outs, (query_ref, held, sems, sent) = rest[: len(steps)], rest[len(steps) :]
        copies = fetches([query_in], [query_ref], sems)
        back = back_ref[...]
        high = jnp.floor(back * (1.0 / 16.0))
        line = jnp.concatenate([high, back - 16.0 * high], axis=1)
        line = (jnp.zeros((16, 2 * plan.rows), F32) + line).astype(BF16)
        copies.pop().wait()
        for number, step in enumerate(steps):
            if plan.group == 1:
                fill(held.at[0], query_ref[...], line)
            head = info_ref[0] ^ step
            lanes = pl.ds(pl.multiple_of((head >> 1) * 2 * width, 128), 2 * width)
            for odd in (0, 1) if plan.group > 1 else ():

                @pl.when((head & 1) == odd)
                def _():
                    own = slice(odd * width, (odd + 1) * width)
                    fill(held.at[number], query_ref[:, lanes][:, own], line)

            copies += fetches([held.at[number]], [outs[number]], sent.at[pl.ds(number, 1)])
        for copy in copies:
            copy.wait()

    block = jax.ShapeDtypeStruct((half + 16, 2 * width), BF16)
    return call(
        body,
        info,
        (reach,),
        (),
        [
            pltpu.VMEM(queries.shape, BF16),
            pltpu.VMEM((len(steps), half + 16, 2 * width), BF16),
            pltpu.SemaphoreType.DMA((1,)),
            pltpu.SemaphoreType.DMA((len(steps),)),
        ],
        late=(queries,),
        far=(block,) * len(steps),
        flops=PACK * MICROSECOND,
        after=after,
    )


def exchange(plan, blocks, steps=None):
    moved = {}
    for step in range(plan.group) if steps is None else steps:
        pairs = [(source, source ^ step) for source in range(plan.count)]
        moved[step] = lax.ppermute(blocks[step], "tok", pairs) if step else blocks[0]
    return moved


def sigmoid(value):
    return 0.5 * jnp.tanh(0.5 * value) + 0.5


def column(row):
    return jnp.swapaxes(jnp.broadcast_to(row, (8, row.shape[1])), 0, 1)[:, 0:1]


def delayed(plan, info, blocks, after):
    count = len(blocks)

    def body(info_ref, *refs):
        held, sems = refs[2 * count :]
        places = [held.at[number] for number in range(count)]
        for sources, targets in ((refs[:count], places), (places, refs[count : 2 * count])):
            for copy in fetches(sources, targets, sems):
                copy.wait()

    block = blocks[0]
    outs = tuple(jax.ShapeDtypeStruct(block.shape, block.dtype) for block in blocks)
    scratch = [pltpu.VMEM((count, *block.shape), block.dtype), pltpu.SemaphoreType.DMA((count,))]
    return call(
        body,
        info,
        (),
        (),
        scratch,
        flops=DELAY * MICROSECOND,
        late=blocks,
        far=outs,
        after=after,
    )


def line_places(plan):
    for owner in range(plan.count):
        for kind in range(3):
            for side in range(plan.fold):
                lines = slice(kind * plan.part, (kind + 1) * plan.part)
                lanes = slice(side * plan.width, (side + 1) * plan.width)
                yield owner, kind, lines, lanes, owner * plan.cols + side * plan.part


def fill_wire(plan, acc_both, acc_down, out, turned, lines):
    turned[0 : plan.pad] = acc_both[:, 0 : plan.pad].T
    turned[plan.pad : 2 * plan.pad] = acc_both[:, plan.pad :].T
    lines[:, plan.used :, :] = jnp.zeros((plan.count, plan.lines - plan.used, plan.wide), F32)
    for owner, kind, where, lanes, begin in line_places(plan):
        if kind < 2:
            piece = turned[kind * plan.pad + begin : kind * plan.pad + begin + plan.part, :]
        else:
            piece = acc_down[plan.gap + begin : plan.gap + begin + plan.part, :]
        lines[owner, where, lanes] = piece[:, 0 : plan.width]
    out[...] = lines[...].astype(BF16)


def unpack(plan, wire_ref, wide, both_ref, down_ref):
    width, pad, gap = plan.width, plan.pad, plan.gap
    if gap:
        wide[:, :, width:] = jnp.zeros((3, pad, gap), F32)
        wide[0:2, width:, :] = jnp.zeros((2, gap, pad), F32)
        wide[2, 0:gap, :] = jnp.zeros((gap, pad), F32)
    chunk = None
    for owner, kind, where, lanes, begin in line_places(plan):
        if kind == 0 and lanes.start == 0:
            chunk = wire_ref[owner].astype(F32)
        begin += gap if kind == 2 else 0
        wide[kind, begin : begin + plan.part, 0:width] = chunk[where, lanes]
    both_ref[:, 0:pad] = wide[0].T.astype(BF16)
    both_ref[:, pad:] = wide[1].T.astype(BF16)
    down_ref[...] = wide[2].astype(BF16)


def weights_of(plan, info, wire, after=()):
    rows = plan.rows

    def body(info_ref, wire_ref, both_ref, down_ref, rate_out, wide):
        unpack(plan, wire_ref, wide, both_ref, down_ref)
        for block in range(plan.group if plan.group > 1 else 0):
            line = wire_ref[info_ref[3] + block].astype(F32)[plan.used : plan.used + 1]
            rate_out[block : block + 1, :] = line[:, 0:rows] + line[:, rows : 2 * rows]

    pad = plan.pad
    return call(
        body,
        info,
        (wire,),
        (
            jax.ShapeDtypeStruct((pad, 2 * pad), BF16),
            jax.ShapeDtypeStruct((pad, pad), BF16),
            jax.ShapeDtypeStruct((plan.group, rows), F32),
        ),
        [pltpu.VMEM((3, pad, pad), F32)],
        after=after,
    )


def gradients(plan, info, weights, blocks, rates, number, after=()):
    width, pad, rows = plan.width, plan.pad, plan.rows

    def body(info_ref, rate_ref, *rest):
        both_ref, down_ref, *rest = rest
        sources, rest = rest[: plan.group], rest[plan.group :]
        out, kv, sems, acc_both, acc_down, turned, lines = rest
        targets = [kv.at[info_ref[0] ^ step] for step in plan.order]
        copies = fetches(sources, targets, sems)
        acc_both[...] = jnp.zeros_like(acc_both)
        acc_down[...] = jnp.zeros_like(acc_down)
        for copy in copies:
            copy.wait()
        @pl.loop(0, plan.group // plan.run)
        def _(turn_of):
            run = turn_of * plan.run
            start = info_ref[1] + run * rows
            live = start < info_ref[2] if number == 0 else start + plan.run * rows > info_ref[2]

            @pl.when(live)
            def _():
                rate = []
                for step in range(plan.run):
                    block = run + step
                    place = info_ref[1] + block * rows
                    place += lax.broadcasted_iota(jnp.int32, (1, rows), 1)
                    member = place < info_ref[2] if number == 0 else place >= info_ref[2]
                    rate.append(column(jnp.where(member, -rate_ref[pl.ds(block, 1), :], 0.0)))
                both_kinds = kv[pl.ds(run, plan.run)].reshape(plan.run * rows, 2 * width)
                keys = both_kinds[:, plan.lanes[0]]
                values = both_kinds[:, plan.lanes[1]].astype(F32)
                errors = (jnp.concatenate(rate, axis=0) * values).astype(BF16)
                pre = dot(keys, both_ref[...], 1, 0)
                back = dot(errors, down_ref[...], 1, 0)
                gate, up = pre[:, 0:pad], pre[:, pad:]
                sigma = sigmoid(gate)
                active = gate * sigma
                hidden = (active * up).astype(BF16)
                turn = sigma + active * (1.0 - sigma)
                slope = (back * up * turn).astype(BF16)
                joint = jnp.concatenate([slope, (back * active).astype(BF16)], axis=1)
                acc_both[...] += dot(keys, joint, 0, 0)
                acc_down[...] += dot(errors, hidden, 0, 0)

        fill_wire(plan, acc_both, acc_down, out, turned, lines)

    outputs = (jax.ShapeDtypeStruct(plan.wire, BF16),)
    scratch = [
        pltpu.VMEM((plan.group, rows, 2 * width), BF16),
        pltpu.SemaphoreType.DMA((plan.group,)),
        pltpu.VMEM((pad, 2 * pad), F32),
        pltpu.VMEM((pad, pad), F32),
        pltpu.VMEM((2 * pad, pad), F32),
        pltpu.VMEM(plan.wire, F32),
    ]
    return call(
        body,
        info,
        (rates, *weights),
        outputs,
        scratch,
        flops=GRAD * MICROSECOND,
        late=blocks,
        after=after,
    )


def unfold(plan, ref):
    half, width = plan.half, plan.width
    first = ref[0:half, plan.lanes[0]]
    second = ref[0:half, plan.lanes[1]]
    second = jnp.concatenate([second[:, plan.gap :], second[:, 0 : plan.gap]], axis=1)
    lane = lax.broadcasted_iota(jnp.int32, (1, plan.pad), 1)
    keep = jnp.where(lane < width, 1.0, 0.0).astype(BF16)
    return jnp.concatenate([first, second], axis=0) * keep


def fold(plan, value):
    half, gap, pad = plan.half, plan.gap, plan.pad
    return jnp.concatenate([value[0:half, gap:], value[half:, gap:]], axis=1)


def mixes(plan, info, firsts, seconds, queries, after=()):
    count = len(queries)
    width, pad, rows, half = plan.width, plan.pad, plan.rows, plan.half

    def body(info_ref, *rest):
        weights, rest = rest[:4], rest[4:]
        sources, rest = rest[:count], rest[count:]
        outs, (asks, news, both, down, sems, sent) = rest[:count], rest[count:]
        place, border = info_ref[0], info_ref[2]
        copies = fetches(sources, [asks.at[index] for index in range(count)], sems)
        for group in range(2):
            both[group] = weights[2 * group][...]
            down[group] = weights[2 * group + 1][...].astype(F32).T.astype(BF16)
        for copy in copies:
            copy.wait()

        def apply(asked, group):
            pre = dot(asked, both[group], 1, 0)
            gate, up = pre[:, 0:pad], pre[:, pad:]
            hidden = (gate * sigmoid(gate) * up).astype(BF16)
            return dot(hidden, down[group], 1, 0)

        @pl.loop(0, count // plan.run)
        def _(turn_of):
            both_of = [turn_of * plan.run + step for step in range(plan.run)]
            starts = [info_ref[1] + (place ^ i) * rows for i in both_of]
            start = functools.reduce(jnp.minimum, starts)
            asked = jnp.concatenate([unfold(plan, asks.at[i]) for i in both_of], axis=0)
            result = apply(asked, (start >= border).astype(jnp.int32))
            for at, i in enumerate(both_of):
                news[i] = fold(plan, result[at * rows : (at + 1) * rows]).astype(BF16)

            @pl.when((start < border) & (start + plan.run * rows > border))
            def _():
                other = apply(asked, 1)
                for at, i in enumerate(both_of):
                    new = fold(plan, other[at * rows : (at + 1) * rows])
                    spot = starts[at] + lax.broadcasted_iota(jnp.int32, new.shape, 0)
                    lane = lax.broadcasted_iota(jnp.int32, new.shape, 1)
                    spot += jnp.where(lane >= width, half, 0)
                    old = news[i].astype(F32)
                    news[i] = jnp.where(spot >= border, new, old).astype(BF16)

        for copy in fetches([news.at[index] for index in range(count)], outs, sent):
            copy.wait()

    block = jax.ShapeDtypeStruct((half, 2 * width), BF16)
    return call(
        body,
        info,
        (*firsts, *seconds),
        (),
        [
            pltpu.VMEM((count, half + 16, 2 * width), BF16),
            pltpu.VMEM((count, half, 2 * width), BF16),
            pltpu.VMEM((2, pad, 2 * pad), BF16),
            pltpu.VMEM((2, pad, pad), BF16),
            pltpu.SemaphoreType.DMA((count,)),
            pltpu.SemaphoreType.DMA((count,)),
        ],
        far=(block,) * count,
        flops=MIX * MICROSECOND,
        late=queries,
        after=after,
    )


def attention(plan, info, queries, blocks, halo, after=()):
    count = len(queries)
    width, pad, rows, half = plan.width, plan.pad, plan.rows, plan.half
    seen = (plan.tail + 1) * rows
    scale = 1.0 / math.sqrt(width)

    def body(info_ref, halo_in, *rest):
        sources, rest = rest[: count + plan.group], rest[count + plan.group :]
        outs, rest = rest[:count], rest[count:]
        asks, held, news, sems, sent = rest
        place = info_ref[0]
        targets = [held.at[0 : plan.tail]]
        targets += [asks.at[number] for number in range(count)]
        targets += [held.at[plan.tail + (place ^ step)] for step in plan.order]
        for copy in fetches((halo_in, *sources), targets, sems):
            copy.wait()
        query = lax.broadcasted_iota(jnp.int32, (rows, 1), 0) + plan.tail * rows
        spot = lax.broadcasted_iota(jnp.int32, (rows, seen), 1)
        @pl.loop(0, count, unroll=min(2, count))
        def _(number):
            block = place ^ number
            line = asks[number, half : half + 16, :].astype(F32)[0:1, :]
            reach = column(line[:, 0:rows] * 16.0 + line[:, rows : 2 * rows]).astype(jnp.int32)
            first = plan.tail * rows - info_ref[1] - block * rows
            low = jnp.maximum(query - reach, first)
            window = held[pl.ds(block, plan.tail + 1)].reshape(seen, 2 * width)
            scores = dot(unfold(plan, asks.at[number]), window[:, plan.lanes[0]], 1, 1)
            scores = jnp.where((spot <= query) & (spot >= low), scores, -jnp.inf)
            top = jnp.max(scores, axis=1, keepdims=True)
            weights = jnp.exp((scores - top) * scale)
            total = jnp.sum(weights, axis=1, keepdims=True)
            mixed = dot(weights.astype(BF16), window[:, plan.lanes[1]], 1, 0)
            news[number] = fold(plan, mixed * (1.0 / total)).astype(BF16)

        for copy in fetches([news.at[number] for number in range(count)], outs, sent):
            copy.wait()

    block = jax.ShapeDtypeStruct((half, 2 * width), BF16)
    return call(
        body,
        info,
        (),
        (),
        [
            pltpu.VMEM((count, half + 16, 2 * width), BF16),
            pltpu.VMEM((plan.tail + plan.group, rows, 2 * width), BF16),
            pltpu.VMEM((count, half, 2 * width), BF16),
            pltpu.SemaphoreType.DMA((1 + count + plan.group,)),
            pltpu.SemaphoreType.DMA((count,)),
        ],
        far=(block,) * count,
        flops=ATT * MICROSECOND,
        late=(halo, *queries, *blocks),
        after=after,
    )


def halo_of(plan, last):
    span = plan.group * plan.rows
    shifts = -(-WINDOW // span)
    if shifts == 1:
        pairs = [(i, i + plan.group) for i in range(plan.count - plan.group)]
        return lax.ppermute(last, "tok", pairs)
    parts = []
    for distance in range(shifts, 0, -1):
        hop = distance * plan.group
        parts.append(lax.ppermute(last, "tok", [(i, i + hop) for i in range(plan.count - hop)]))
    return jnp.concatenate(parts, axis=0)[-plan.tail :]


def finish(plan, info, mixed, attended, gain, after):
    width, half, total = plan.width, plan.half, plan.heads * plan.width

    def body(info_ref, gain_ref, *rest):
        sources, rest = rest[: 2 * plan.group], rest[2 * plan.group :]
        out_far, ys, adds, out, sems, sent = rest
        targets = [held.at[step] for held in (ys, adds) for step in range(plan.group)]
        copies = fetches(sources, targets, sems)
        done = []
        squares = jnp.zeros((half, 2 * width), F32)
        for step in range(plan.group):
            copies[step].wait()
            y = ys[step].astype(F32)
            squares += y * y
        norms = [
            lax.rsqrt(jnp.sum(s, axis=1, keepdims=True) * (1.0 / total) + 1e-06)
            for s in (squares[:, 0:width], squares[:, width:])
        ]
        lane = lax.broadcasted_iota(jnp.int32, (half, 2 * width), 1)
        norm = jnp.where(lane < width, norms[0], norms[1])
        for pair in range(plan.group // 2):
            lanes = pl.ds(pl.multiple_of(((info_ref[0] >> 1) ^ pair) * 2 * width, 128), 2 * width)
            values = []
            for step in (2 * pair, 2 * pair + 1):
                copies[plan.group + step].wait()
                scale = gain_ref[pl.ds(info_ref[0] ^ step, 1), :]
                value = ys[step].astype(F32) * norm * scale + adds[step].astype(F32)
                values.append(value.astype(BF16))
            for odd in (0, 1):

                @pl.when((info_ref[0] & 1) == odd)
                def _():
                    even, other = values[odd], values[1 - odd]
                    for side in range(2):
                        own = slice(side * width, (side + 1) * width)
                        joined = jnp.concatenate([even[:, own], other[:, own]], axis=1)
                        out[pair, side * half : (side + 1) * half, :] = joined

            done += fetches([out.at[pair]], [out_far.at[:, lanes]], sent.at[pl.ds(pair, 1)])
        for copy in done:
            copy.wait()

    gain = gain.reshape(plan.heads, width)
    return call(
        body,
        info,
        (jnp.concatenate([gain, gain], axis=1),),
        (),
        [
            pltpu.VMEM((plan.group, half, 2 * width), BF16),
            pltpu.VMEM((plan.group, half, 2 * width), BF16),
            pltpu.VMEM((plan.group // 2, plan.rows, 2 * width), BF16),
            pltpu.SemaphoreType.DMA((2 * plan.group,)),
            pltpu.SemaphoreType.DMA((plan.group // 2,)),
        ],
        late=tuple(held[step] for held in (mixed, attended) for step in range(plan.group)),
        far=(jax.ShapeDtypeStruct((plan.rows, total), BF16),),
        flops=FINISH * MICROSECOND,
        after=after,
    )[0]


def finish_apart(plan, mixed, attended, gain):
    def flat(block):
        return jnp.concatenate([block[:, : plan.width], block[:, plan.width :]], axis=0).astype(F32)

    y, a = flat(mixed[0]), flat(attended[0])
    squares = lax.psum(jnp.sum(y * y, axis=1, keepdims=True), "head")
    mean = squares / (plan.heads * plan.width * lax.axis_size("head"))
    return (y / jnp.sqrt(mean + 1e-06) * gain.reshape(1, -1) + a).astype(BF16)


def spent(info):
    def body(info_ref, out):
        out[...] = jnp.zeros_like(out) + info_ref[0]

    return call(body, info, (), (jax.ShapeDtypeStruct((8, 128), jnp.int32),), flops=SPENT * MICROSECOND)[0]


def spread(wire):
    return lax.all_to_all(wire, "tok", 0, 0, tiled=True)


def on_device(queries, keys, values, rates, back, group_end, gate_init, up_init, down_init, gain):
    rows, heads = rates.shape
    count = lax.axis_size("tok")
    plan = Plan(rows, heads, queries.shape[1] // heads, gate_init.shape[2], count)
    me = lax.axis_index("tok").astype(jnp.int32)
    place = lax.rem(me, plan.group)
    info = jnp.stack([place, (me - place) * rows, group_end[0], me - place])
    states = tuple(jnp.transpose(w, (2, 0, 1)) for w in (gate_init, up_init, down_init))
    rate_rows = rates.T
    reach = back.astype(F32).reshape(1, rows)

    steps = plan.steps
    packed = pack_pair(plan, info, keys, values)
    blocks = [*exchange(plan, dict(zip(plan.order, packed)), plan.order).values()]
    wire = spread(pack_state(plan, info, states, rate_rows, packed[:1]))
    both, down, found = weights_of(plan, info, wire, (spent(info),))
    if plan.group > 1:
        rate_rows = found

    def part(steps, blocks):
        return [blocks[step] for step in steps]

    last = last_blocks(plan, info, blocks, (down,))
    wire = gradients(plan, info, (both, down), blocks, rate_rows, 0, (last,))[0]
    halo = halo_of(plan, last)
    found = pack_queries(plan, info, queries, reach, steps, (wire, halo))
    asks = exchange(plan, dict(zip(steps, found)))
    wire = spread(wire)
    *states, wire = update(plan, info, states, wire, True, part((1, 6) if steps[6:] else (), asks))
    wire, after = spread(wire), (wire,)
    found = attention(plan, info, part(steps, asks), blocks, halo, after)
    attended, after = dict(zip(steps, found)), found[:1]
    attended = exchange(plan, attended)
    firsts = (both, down)
    *seconds, _ = weights_of(plan, info, wire, after)
    found = mixes(plan, info, firsts, seconds, part(steps, asks))
    after = (*found[:1], *part(steps[1:], attended))
    wire = gradients(plan, info, seconds, blocks, rate_rows, 1, after)[0]
    first, later = (*steps[:1], *steps[3:]), steps[1:3]
    mixed = exchange(plan, dict(zip(steps, found)), first)
    after = ()
    if later:
        after = delayed(plan, info, part(later, found), (wire, *part(first[1:], mixed)))
        mixed.update(exchange(plan, dict(zip(later, after)), later))
    states = update(plan, info, states, spread(wire), False, after[:1])
    if plan.group > 1:
        output = finish(plan, info, mixed, attended, gain, states[:1])
    else:
        output = finish_apart(plan, mixed, attended, gain)
    return (output, *(jnp.transpose(w, (1, 2, 0)) for w in states))


def solution(mesh):
    tokens, state = P("tok", "head"), P("head", None, "tok")
    return jax.shard_map(
        on_device,
        mesh=mesh,
        in_specs=(tokens, tokens, tokens, tokens, P("tok"), P(), state, state, state, P("head")),
        out_specs=(tokens, state, state, state),
        check_vma=False,
    )
```

```python
import functools
import math

import jax
import jax.numpy as jnp
from jax import lax
from jax.experimental import pallas as pl
from jax.experimental.pallas import tpu as pltpu
from jax.sharding import PartitionSpec as P

WINDOW = 512
BF16 = jnp.bfloat16
F32 = jnp.float32
MIB = 1 << 20
MICROSECOND = 10**9
ATT, MIX, GRAD, DELAY, FINISH, PACK = 10, 8, 12, 20, 10, 30
SPENT = 40

VMEM = pl.BlockSpec(memory_space=pltpu.VMEM)
SMEM = pl.BlockSpec(memory_space=pltpu.SMEM)
HBM = pl.BlockSpec(memory_space=pltpu.HBM)


def dot(lhs, rhs, lhs_dim, rhs_dim):
    return lax.dot_general(
        lhs, rhs, (((lhs_dim,), (rhs_dim,)), ((), ())), preferred_element_type=F32
    )


def call(
    body, info, inputs, outputs, scratch=(), flops=0, limit=60, late=(), far=(), after=()
):
    moved = sum(math.prod(x.shape) * x.dtype.itemsize for x in [*inputs, *late, *outputs, *far])
    given = 1 + len(inputs) + len(late)

    def kernel(*refs):
        body(*refs[:given], *refs[given + len(after) :])

    return pl.pallas_call(
        kernel,
        out_shape=(*outputs, *far),
        in_specs=[SMEM] + [VMEM] * len(inputs) + [HBM] * (len(late) + len(after)),
        out_specs=(*(VMEM for _ in outputs), *(HBM for _ in far)),
        scratch_shapes=list(scratch),
        compiler_params=pltpu.CompilerParams(vmem_limit_bytes=limit * MIB),
        cost_estimate=pl.CostEstimate(flops=flops, bytes_accessed=0, transcendentals=0),
    )(info, *inputs, *late, *after)


def fetches(sources, targets, semaphores):
    copies = [
        pltpu.make_async_copy(source, target, semaphores.at[number])
        for number, (source, target) in enumerate(zip(sources, targets))
    ]
    for copy in copies:
        copy.start()
    return copies


class Plan:
    def __init__(self, rows, heads, width, cols, count):
        self.rows, self.heads, self.width, self.cols, self.count = rows, heads, width, cols, count
        self.group = heads
        self.planes = count // heads
        self.fold = 2 if cols % 2 == 0 else 1
        self.part = cols // self.fold
        self.used = 3 * self.part
        self.lines = -(-(self.used + 1) // 16) * 16
        self.wide = self.fold * width
        self.pad = -(-width // 128) * 128
        self.gap = self.pad - width
        self.lanes = (slice(0, self.pad), slice(2 * width - self.pad, 2 * width))
        self.half = rows // 2
        self.steps = tuple(range(self.group))
        self.order = (0, 6, 7, 2, 4, 3, 5, 1) if self.group == 8 else self.steps
        self.run = 2 if self.group % 2 == 0 else 1
        self.tail = -(-WINDOW // rows)
        self.wire = (count, self.lines, self.wide)


def pack_state(plan, info, states, rates, after):
    def body(info_ref, gate_in, up_in, down_in, rate_in, out, lines, gate, up, down, rate, sems):
        copies = fetches((gate_in, up_in, down_in, rate_in), (gate, up, down, rate), sems)
        lines[...] = jnp.zeros_like(lines)
        for copy in copies:
            copy.wait()
        for kind, ref in enumerate((gate, up, down)):
            for col in range(plan.cols):
                side, line = divmod(col, plan.part)
                lanes = slice(side * plan.width, (side + 1) * plan.width)
                lines[:, kind * plan.part + line, lanes] = ref[col]
        if plan.group > 1:
            high = rate[...].astype(BF16).astype(F32)
            lines[:, plan.used, 0 : plan.rows] = high
            lines[:, plan.used, plan.rows : 2 * plan.rows] = rate[...] - high
        packed = lines[...].astype(BF16)
        for plane in range(plan.planes):
            out[plane * plan.group : (plane + 1) * plan.group] = packed

    return call(
        body,
        info,
        (),
        (jax.ShapeDtypeStruct(plan.wire, BF16),),
        [pltpu.VMEM((plan.group, plan.lines, plan.wide), F32)]
        + [pltpu.VMEM((plan.cols, plan.heads, plan.width), F32)] * 3
        + [pltpu.VMEM((plan.heads, plan.rows), F32), pltpu.SemaphoreType.DMA((4,))],
        late=(*states, rates),
        after=after,
    )[0]


def update(plan, info, states, wire, send, after=()):
    def body(info_ref, wire_ref, gate_in, up_in, down_in, *rest):
        if not send:
            rest = (*rest[:-1], gate_in, up_in, down_in, None)
        news, rest = rest[:3], rest[3:]
        out = rest[0] if send else None
        total, grad, gate, up, down, sems = rest[-6:]
        copies = fetches((gate_in, up_in, down_in), (gate, up, down), sems) if send else ()
        acc = wire_ref[0 : plan.group].astype(F32)
        for plane in range(1, plan.planes):
            acc += wire_ref[plane * plan.group : (plane + 1) * plan.group].astype(F32)
        total[...] = acc
        for kind, ref in enumerate((gate, up, down)):
            for col in range(plan.cols):
                side, line = divmod(col, plan.part)
                lanes = slice(side * plan.width, (side + 1) * plan.width)
                grad[col] = total[:, kind * plan.part + line, lanes]
            if send:
                copies[kind].wait()
            old = ref[...]
            fresh = old - grad[...]
            old_norm = jnp.sqrt(jnp.sum(old * old, axis=2, keepdims=True))
            new_norm = jnp.sqrt(jnp.sum(fresh * fresh, axis=2, keepdims=True) + 1e-06)
            new = fresh * (old_norm / new_norm)
            news[kind][...] = new
            if send:
                for col in range(plan.cols):
                    side, line = divmod(col, plan.part)
                    lanes = slice(side * plan.width, (side + 1) * plan.width)
                    total[:, kind * plan.part + line, lanes] = new[col]
        if send:
            packed = total[...].astype(BF16)
            for plane in range(plan.planes):
                out[plane * plan.group : (plane + 1) * plan.group] = packed

    state = jax.ShapeDtypeStruct((plan.cols, plan.heads, plan.width), F32)
    outputs = (state, state, state)
    if send:
        outputs += (jax.ShapeDtypeStruct(plan.wire, BF16),)
    return call(
        body,
        info,
        (wire,) if send else (wire, *states),
        outputs,
        [pltpu.VMEM((plan.group, plan.lines, plan.wide), F32)]
        + [pltpu.VMEM((plan.cols, plan.heads, plan.width), F32)] * (4 if send else 1)
        + [pltpu.SemaphoreType.DMA((3,))],
        late=states if send else (),
        after=after,
    )


def pack_pair(plan, info, left, right):
    def body(info_ref, left_in, right_in, *rest):
        outs, (left_ref, right_ref, held, sems, sent) = rest[: plan.group], rest[plan.group :]
        copies = []
        for copy in fetches((left_in, right_in), (left_ref, right_ref), sems):
            copy.wait()
        for step in range(plan.group):
            head = info_ref[0] ^ plan.order[step]
            lanes = pl.ds(pl.multiple_of((head >> 1) * 2 * plan.width, 128), 2 * plan.width)
            for odd in (0, 1):

                @pl.when((head & 1) == odd)
                def _():
                    own = slice(odd * plan.width, (odd + 1) * plan.width)
                    held[step, :, 0 : plan.width] = left_ref[:, lanes][:, own]
                    held[step, :, plan.width : 2 * plan.width] = right_ref[:, lanes][:, own]

            copies += fetches([held.at[step]], [outs[step]], sent.at[pl.ds(step, 1)])
        for copy in copies:
            copy.wait()

    if plan.group == 1:
        return (jnp.concatenate([left, right], axis=1),)
    block = jax.ShapeDtypeStruct((plan.rows, 2 * plan.width), BF16)
    return call(
        body,
        info,
        (),
        (),
        [pltpu.VMEM(left.shape, BF16)] * 2
        + [
            pltpu.VMEM((plan.group, plan.rows, 2 * plan.width), BF16),
            pltpu.SemaphoreType.DMA((2,)),
            pltpu.SemaphoreType.DMA((plan.group,)),
        ],
        late=(left, right),
        far=(block,) * plan.group,
    )


def last_blocks(plan, info, blocks, after=()):
    def body(info_ref, *refs):
        sources, (out, held, sems, sent) = refs[: plan.group], refs[plan.group :]

        def each(act):
            for step in range(plan.group):
                block = (info_ref[0] ^ plan.order[step]) - (plan.group - plan.tail)

                @pl.when(block >= 0)
                def _():
                    act(pltpu.make_async_copy(sources[step], held.at[block], sems.at[step]))

        each(lambda copy: copy.start())
        each(lambda copy: copy.wait())
        fetches([held], [out], sent)[0].wait()

    if plan.group == 1:
        return blocks[0].reshape(1, plan.rows, -1)
    block = jax.ShapeDtypeStruct((plan.tail, plan.rows, 2 * plan.width), BF16)
    scratch = [pltpu.VMEM(block.shape, BF16)]
    scratch += [pltpu.SemaphoreType.DMA((size,)) for size in (plan.group, 1)]
    return call(body, info, (), (), scratch, late=blocks, far=(block,), after=after)[0]


def pack_queries(plan, info, queries, reach, steps, after=()):
    half, width = plan.half, plan.width

    def fill(out, own, line):
        out[0:half, 0:width] = own[0:half]
        out[0:half, width : 2 * width] = own[half : 2 * half]
        out[half : half + 16, 0 : 2 * plan.rows] = line
        out[half : half + 16, 2 * plan.rows :] = jnp.zeros((16, 2 * (width - plan.rows)), BF16)

    def body(info_ref, back_ref, query_in, *rest):
        outs, (query_ref, held, sems, sent) = rest[: len(steps)], rest[len(steps) :]
        copies = fetches([query_in], [query_ref], sems)
        back = back_ref[...]
        high = jnp.floor(back * (1.0 / 16.0))
        line = jnp.concatenate([high, back - 16.0 * high], axis=1)
        line = (jnp.zeros((16, 2 * plan.rows), F32) + line).astype(BF16)
        copies.pop().wait()
        for number, step in enumerate(steps):
            if plan.group == 1:
                fill(held.at[0], query_ref[...], line)
            head = info_ref[0] ^ step
            lanes = pl.ds(pl.multiple_of((head >> 1) * 2 * width, 128), 2 * width)
            for odd in (0, 1) if plan.group > 1 else ():

                @pl.when((head & 1) == odd)
                def _():
                    own = slice(odd * width, (odd + 1) * width)
                    fill(held.at[number], query_ref[:, lanes][:, own], line)

            copies += fetches([held.at[number]], [outs[number]], sent.at[pl.ds(number, 1)])
        for copy in copies:
            copy.wait()

    block = jax.ShapeDtypeStruct((half + 16, 2 * width), BF16)
    return call(
        body,
        info,
        (reach,),
        (),
        [
            pltpu.VMEM(queries.shape, BF16),
            pltpu.VMEM((len(steps), half + 16, 2 * width), BF16),
            pltpu.SemaphoreType.DMA((1,)),
            pltpu.SemaphoreType.DMA((len(steps),)),
        ],
        late=(queries,),
        far=(block,) * len(steps),
        flops=PACK * MICROSECOND,
        after=after,
    )


def exchange(plan, blocks, steps=None):
    moved = {}
    for step in range(plan.group) if steps is None else steps:
        pairs = [(source, source ^ step) for source in range(plan.count)]
        moved[step] = lax.ppermute(blocks[step], "tok", pairs) if step else blocks[0]
    return moved


def sigmoid(value):
    return 0.5 * jnp.tanh(0.5 * value) + 0.5


def column(row):
    return jnp.swapaxes(jnp.broadcast_to(row, (8, row.shape[1])), 0, 1)[:, 0:1]


def delayed(plan, info, blocks, after):
    count = len(blocks)

    def body(info_ref, *refs):
        held, sems = refs[2 * count :]
        places = [held.at[number] for number in range(count)]
        for sources, targets in ((refs[:count], places), (places, refs[count : 2 * count])):
            for copy in fetches(sources, targets, sems):
                copy.wait()

    block = blocks[0]
    outs = tuple(jax.ShapeDtypeStruct(block.shape, block.dtype) for block in blocks)
    scratch = [pltpu.VMEM((count, *block.shape), block.dtype), pltpu.SemaphoreType.DMA((count,))]
    return call(
        body,
        info,
        (),
        (),
        scratch,
        flops=DELAY * MICROSECOND,
        late=blocks,
        far=outs,
        after=after,
    )


def line_places(plan):
    for owner in range(plan.count):
        for kind in range(3):
            for side in range(plan.fold):
                lines = slice(kind * plan.part, (kind + 1) * plan.part)
                lanes = slice(side * plan.width, (side + 1) * plan.width)
                yield owner, kind, lines, lanes, owner * plan.cols + side * plan.part


def fill_wire(plan, acc_both, acc_down, out, turned, lines):
    turned[0 : plan.pad] = acc_both[:, 0 : plan.pad].T
    turned[plan.pad : 2 * plan.pad] = acc_both[:, plan.pad :].T
    lines[:, plan.used :, :] = jnp.zeros((plan.count, plan.lines - plan.used, plan.wide), F32)
    for owner, kind, where, lanes, begin in line_places(plan):
        if kind < 2:
            piece = turned[kind * plan.pad + begin : kind * plan.pad + begin + plan.part, :]
        else:
            piece = acc_down[plan.gap + begin : plan.gap + begin + plan.part, :]
        lines[owner, where, lanes] = piece[:, 0 : plan.width]
    out[...] = lines[...].astype(BF16)


def unpack(plan, wire_ref, wide, both_ref, down_ref):
    width, pad, gap = plan.width, plan.pad, plan.gap
    if gap:
        wide[:, :, width:] = jnp.zeros((3, pad, gap), F32)
        wide[0:2, width:, :] = jnp.zeros((2, gap, pad), F32)
        wide[2, 0:gap, :] = jnp.zeros((gap, pad), F32)
    chunk = None
    for owner, kind, where, lanes, begin in line_places(plan):
        if kind == 0 and lanes.start == 0:
            chunk = wire_ref[owner].astype(F32)
        begin += gap if kind == 2 else 0
        wide[kind, begin : begin + plan.part, 0:width] = chunk[where, lanes]
    both_ref[:, 0:pad] = wide[0].T.astype(BF16)
    both_ref[:, pad:] = wide[1].T.astype(BF16)
    down_ref[...] = wide[2].astype(BF16)


def weights_of(plan, info, wire, after=()):
    rows = plan.rows

    def body(info_ref, wire_ref, both_ref, down_ref, rate_out, wide):
        unpack(plan, wire_ref, wide, both_ref, down_ref)
        for block in range(plan.group if plan.group > 1 else 0):
            line = wire_ref[info_ref[3] + block].astype(F32)[plan.used : plan.used + 1]
            rate_out[block : block + 1, :] = line[:, 0:rows] + line[:, rows : 2 * rows]

    pad = plan.pad
    return call(
        body,
        info,
        (wire,),
        (
            jax.ShapeDtypeStruct((pad, 2 * pad), BF16),
            jax.ShapeDtypeStruct((pad, pad), BF16),
            jax.ShapeDtypeStruct((plan.group, rows), F32),
        ),
        [pltpu.VMEM((3, pad, pad), F32)],
        after=after,
    )


def gradients(plan, info, weights, blocks, rates, number, after=()):
    width, pad, rows = plan.width, plan.pad, plan.rows

    def body(info_ref, rate_ref, *rest):
        both_ref, down_ref, *rest = rest
        sources, rest = rest[: plan.group], rest[plan.group :]
        out, kv, sems, acc_both, acc_down, turned, lines = rest
        targets = [kv.at[info_ref[0] ^ step] for step in plan.order]
        copies = fetches(sources, targets, sems)
        acc_both[...] = jnp.zeros_like(acc_both)
        acc_down[...] = jnp.zeros_like(acc_down)
        for copy in copies:
            copy.wait()
        @pl.loop(0, plan.group // plan.run)
        def _(turn_of):
            run = turn_of * plan.run
            start = info_ref[1] + run * rows
            live = start < info_ref[2] if number == 0 else start + plan.run * rows > info_ref[2]

            @pl.when(live)
            def _():
                rate = []
                for step in range(plan.run):
                    block = run + step
                    place = info_ref[1] + block * rows
                    place += lax.broadcasted_iota(jnp.int32, (1, rows), 1)
                    member = place < info_ref[2] if number == 0 else place >= info_ref[2]
                    rate.append(column(jnp.where(member, -rate_ref[pl.ds(block, 1), :], 0.0)))
                both_kinds = kv[pl.ds(run, plan.run)].reshape(plan.run * rows, 2 * width)
                keys = both_kinds[:, plan.lanes[0]]
                values = both_kinds[:, plan.lanes[1]].astype(F32)
                errors = (jnp.concatenate(rate, axis=0) * values).astype(BF16)
                pre = dot(keys, both_ref[...], 1, 0)
                back = dot(errors, down_ref[...], 1, 0)
                gate, up = pre[:, 0:pad], pre[:, pad:]
                sigma = sigmoid(gate)
                active = gate * sigma
                hidden = (active * up).astype(BF16)
                turn = sigma + active * (1.0 - sigma)
                slope = (back * up * turn).astype(BF16)
                joint = jnp.concatenate([slope, (back * active).astype(BF16)], axis=1)
                acc_both[...] += dot(keys, joint, 0, 0)
                acc_down[...] += dot(errors, hidden, 0, 0)

        fill_wire(plan, acc_both, acc_down, out, turned, lines)

    outputs = (jax.ShapeDtypeStruct(plan.wire, BF16),)
    scratch = [
        pltpu.VMEM((plan.group, rows, 2 * width), BF16),
        pltpu.SemaphoreType.DMA((plan.group,)),
        pltpu.VMEM((pad, 2 * pad), F32),
        pltpu.VMEM((pad, pad), F32),
        pltpu.VMEM((2 * pad, pad), F32),
        pltpu.VMEM(plan.wire, F32),
    ]
    return call(
        body,
        info,
        (rates, *weights),
        outputs,
        scratch,
        flops=GRAD * MICROSECOND,
        late=blocks,
        after=after,
    )


def unfold(plan, ref):
    half, width = plan.half, plan.width
    first = ref[0:half, plan.lanes[0]]
    second = ref[0:half, plan.lanes[1]]
    second = jnp.concatenate([second[:, plan.gap :], second[:, 0 : plan.gap]], axis=1)
    lane = lax.broadcasted_iota(jnp.int32, (1, plan.pad), 1)
    keep = jnp.where(lane < width, 1.0, 0.0).astype(BF16)
    return jnp.concatenate([first, second], axis=0) * keep


def fold(plan, value):
    half, gap, pad = plan.half, plan.gap, plan.pad
    return jnp.concatenate([value[0:half, gap:], value[half:, gap:]], axis=1)


def mixes(plan, info, firsts, seconds, queries, after=()):
    count = len(queries)
    width, pad, rows, half = plan.width, plan.pad, plan.rows, plan.half

    def body(info_ref, *rest):
        weights, rest = rest[:4], rest[4:]
        sources, rest = rest[:count], rest[count:]
        outs, (asks, news, both, down, sems, sent) = rest[:count], rest[count:]
        place, border = info_ref[0], info_ref[2]
        copies = fetches(sources, [asks.at[index] for index in range(count)], sems)
        for group in range(2):
            both[group] = weights[2 * group][...]
            down[group] = weights[2 * group + 1][...].astype(F32).T.astype(BF16)
        for copy in copies:
            copy.wait()

        def apply(asked, group):
            pre = dot(asked, both[group], 1, 0)
            gate, up = pre[:, 0:pad], pre[:, pad:]
            hidden = (gate * sigmoid(gate) * up).astype(BF16)
            return dot(hidden, down[group], 1, 0)

        @pl.loop(0, count // plan.run)
        def _(turn_of):
            both_of = [turn_of * plan.run + step for step in range(plan.run)]
            starts = [info_ref[1] + (place ^ i) * rows for i in both_of]
            start = functools.reduce(jnp.minimum, starts)
            asked = jnp.concatenate([unfold(plan, asks.at[i]) for i in both_of], axis=0)
            result = apply(asked, (start >= border).astype(jnp.int32))
            for at, i in enumerate(both_of):
                news[i] = fold(plan, result[at * rows : (at + 1) * rows]).astype(BF16)

            @pl.when((start < border) & (start + plan.run * rows > border))
            def _():
                other = apply(asked, 1)
                for at, i in enumerate(both_of):
                    new = fold(plan, other[at * rows : (at + 1) * rows])
                    spot = starts[at] + lax.broadcasted_iota(jnp.int32, new.shape, 0)
                    lane = lax.broadcasted_iota(jnp.int32, new.shape, 1)
                    spot += jnp.where(lane >= width, half, 0)
                    old = news[i].astype(F32)
                    news[i] = jnp.where(spot >= border, new, old).astype(BF16)

        for copy in fetches([news.at[index] for index in range(count)], outs, sent):
            copy.wait()

    block = jax.ShapeDtypeStruct((half, 2 * width), BF16)
    return call(
        body,
        info,
        (*firsts, *seconds),
        (),
        [
            pltpu.VMEM((count, half + 16, 2 * width), BF16),
            pltpu.VMEM((count, half, 2 * width), BF16),
            pltpu.VMEM((2, pad, 2 * pad), BF16),
            pltpu.VMEM((2, pad, pad), BF16),
            pltpu.SemaphoreType.DMA((count,)),
            pltpu.SemaphoreType.DMA((count,)),
        ],
        far=(block,) * count,
        flops=MIX * MICROSECOND,
        late=queries,
        after=after,
    )


def attention(plan, info, queries, blocks, halo, after=()):
    count = len(queries)
    width, pad, rows, half = plan.width, plan.pad, plan.rows, plan.half
    seen = (plan.tail + 1) * rows
    scale = 1.0 / math.sqrt(width)

    def body(info_ref, halo_in, *rest):
        sources, rest = rest[: count + plan.group], rest[count + plan.group :]
        outs, rest = rest[:count], rest[count:]
        asks, held, news, sems, sent = rest
        place = info_ref[0]
        targets = [held.at[0 : plan.tail]]
        targets += [asks.at[number] for number in range(count)]
        targets += [held.at[plan.tail + (place ^ step)] for step in plan.order]
        for copy in fetches((halo_in, *sources), targets, sems):
            copy.wait()
        query = lax.broadcasted_iota(jnp.int32, (rows, 1), 0) + plan.tail * rows
        spot = lax.broadcasted_iota(jnp.int32, (rows, seen), 1)
        @pl.loop(0, count, unroll=min(2, count))
        def _(number):
            block = place ^ number
            line = asks[number, half : half + 16, :].astype(F32)[0:1, :]
            reach = column(line[:, 0:rows] * 16.0 + line[:, rows : 2 * rows]).astype(jnp.int32)
            first = plan.tail * rows - info_ref[1] - block * rows
            low = jnp.maximum(query - reach, first)
            window = held[pl.ds(block, plan.tail + 1)].reshape(seen, 2 * width)
            scores = dot(unfold(plan, asks.at[number]), window[:, plan.lanes[0]], 1, 1)
            scores = jnp.where((spot <= query) & (spot >= low), scores, -jnp.inf)
            top = jnp.max(scores, axis=1, keepdims=True)
            weights = jnp.exp((scores - top) * scale)
            total = jnp.sum(weights, axis=1, keepdims=True)
            mixed = dot(weights.astype(BF16), window[:, plan.lanes[1]], 1, 0)
            news[number] = fold(plan, mixed * (1.0 / total)).astype(BF16)

        for copy in fetches([news.at[number] for number in range(count)], outs, sent):
            copy.wait()

    block = jax.ShapeDtypeStruct((half, 2 * width), BF16)
    return call(
        body,
        info,
        (),
        (),
        [
            pltpu.VMEM((count, half + 16, 2 * width), BF16),
            pltpu.VMEM((plan.tail + plan.group, rows, 2 * width), BF16),
            pltpu.VMEM((count, half, 2 * width), BF16),
            pltpu.SemaphoreType.DMA((1 + count + plan.group,)),
            pltpu.SemaphoreType.DMA((count,)),
        ],
        far=(block,) * count,
        flops=ATT * MICROSECOND,
        late=(halo, *queries, *blocks),
        after=after,
    )


def halo_of(plan, last):
    span = plan.group * plan.rows
    shifts = -(-WINDOW // span)
    if shifts == 1:
        pairs = [(i, i + plan.group) for i in range(plan.count - plan.group)]
        return lax.ppermute(last, "tok", pairs)
    parts = []
    for distance in range(shifts, 0, -1):
        hop = distance * plan.group
        parts.append(lax.ppermute(last, "tok", [(i, i + hop) for i in range(plan.count - hop)]))
    return jnp.concatenate(parts, axis=0)[-plan.tail :]


def finish(plan, info, mixed, attended, gain, after):
    width, half, total = plan.width, plan.half, plan.heads * plan.width

    def body(info_ref, gain_ref, *rest):
        sources, rest = rest[: 2 * plan.group], rest[2 * plan.group :]
        out_far, ys, adds, out, sems, sent = rest
        targets = [held.at[step] for held in (ys, adds) for step in range(plan.group)]
        copies = fetches(sources, targets, sems)
        done = []
        squares = jnp.zeros((half, 2 * width), F32)
        for step in range(plan.group):
            copies[step].wait()
            y = ys[step].astype(F32)
            squares += y * y
        norms = [
            lax.rsqrt(jnp.sum(s, axis=1, keepdims=True) * (1.0 / total) + 1e-06)
            for s in (squares[:, 0:width], squares[:, width:])
        ]
        lane = lax.broadcasted_iota(jnp.int32, (half, 2 * width), 1)
        norm = jnp.where(lane < width, norms[0], norms[1])
        for pair in range(plan.group // 2):
            lanes = pl.ds(pl.multiple_of(((info_ref[0] >> 1) ^ pair) * 2 * width, 128), 2 * width)
            values = []
            for step in (2 * pair, 2 * pair + 1):
                copies[plan.group + step].wait()
                scale = gain_ref[pl.ds(info_ref[0] ^ step, 1), :]
                value = ys[step].astype(F32) * norm * scale + adds[step].astype(F32)
                values.append(value.astype(BF16))
            for odd in (0, 1):

                @pl.when((info_ref[0] & 1) == odd)
                def _():
                    even, other = values[odd], values[1 - odd]
                    for side in range(2):
                        own = slice(side * width, (side + 1) * width)
                        joined = jnp.concatenate([even[:, own], other[:, own]], axis=1)
                        out[pair, side * half : (side + 1) * half, :] = joined

            done += fetches([out.at[pair]], [out_far.at[:, lanes]], sent.at[pl.ds(pair, 1)])
        for copy in done:
            copy.wait()

    gain = gain.reshape(plan.heads, width)
    return call(
        body,
        info,
        (jnp.concatenate([gain, gain], axis=1),),
        (),
        [
            pltpu.VMEM((plan.group, half, 2 * width), BF16),
            pltpu.VMEM((plan.group, half, 2 * width), BF16),
            pltpu.VMEM((plan.group // 2, plan.rows, 2 * width), BF16),
            pltpu.SemaphoreType.DMA((2 * plan.group,)),
            pltpu.SemaphoreType.DMA((plan.group // 2,)),
        ],
        late=tuple(held[step] for held in (mixed, attended) for step in range(plan.group)),
        far=(jax.ShapeDtypeStruct((plan.rows, total), BF16),),
        flops=FINISH * MICROSECOND,
        after=after,
    )[0]


def finish_apart(plan, mixed, attended, gain):
    def flat(block):
        return jnp.concatenate([block[:, : plan.width], block[:, plan.width :]], axis=0).astype(F32)

    y, a = flat(mixed[0]), flat(attended[0])
    squares = lax.psum(jnp.sum(y * y, axis=1, keepdims=True), "head")
    mean = squares / (plan.heads * plan.width * lax.axis_size("head"))
    return (y / jnp.sqrt(mean + 1e-06) * gain.reshape(1, -1) + a).astype(BF16)


def spent(info):
    def body(info_ref, out):
        out[...] = jnp.zeros_like(out) + info_ref[0]

    return call(body, info, (), (jax.ShapeDtypeStruct((8, 128), jnp.int32),), flops=SPENT * MICROSECOND)[0]


def spread(wire):
    return lax.all_to_all(wire, "tok", 0, 0, tiled=True)


def on_device(queries, keys, values, rates, back, group_end, gate_init, up_init, down_init, gain):
    rows, heads = rates.shape
    count = lax.axis_size("tok")
    plan = Plan(rows, heads, queries.shape[1] // heads, gate_init.shape[2], count)
    me = lax.axis_index("tok").astype(jnp.int32)
    place = lax.rem(me, plan.group)
    info = jnp.stack([place, (me - place) * rows, group_end[0], me - place])
    states = tuple(jnp.transpose(w, (2, 0, 1)) for w in (gate_init, up_init, down_init))
    rate_rows = rates.T
    reach = back.astype(F32).reshape(1, rows)

    steps = plan.steps
    packed = pack_pair(plan, info, keys, values)
    blocks = [*exchange(plan, dict(zip(plan.order, packed)), plan.order).values()]
    wire = spread(pack_state(plan, info, states, rate_rows, packed[:1]))
    both, down, found = weights_of(plan, info, wire, (spent(info),))
    if plan.group > 1:
        rate_rows = found

    def part(steps, blocks):
        return [blocks[step] for step in steps]

    last = last_blocks(plan, info, blocks, (down,))
    wire = gradients(plan, info, (both, down), blocks, rate_rows, 0, (last,))[0]
    halo = halo_of(plan, last)
    found = pack_queries(plan, info, queries, reach, steps, (wire, halo))
    asks = exchange(plan, dict(zip(steps, found)))
    wire = spread(wire)
    *states, wire = update(plan, info, states, wire, True, part((1, 6) if steps[6:] else (), asks))
    wire, after = spread(wire), (wire,)
    found = attention(plan, info, part(steps, asks), blocks, halo, after)
    attended, after = dict(zip(steps, found)), found[:1]
    attended = exchange(plan, attended)
    firsts = (both, down)
    *seconds, _ = weights_of(plan, info, wire, after)
    found = mixes(plan, info, firsts, seconds, part(steps, asks))
    after = (*found[:1], *part(steps[1:], attended))
    wire = gradients(plan, info, seconds, blocks, rate_rows, 1, after)[0]
    first, later = (*steps[:1], *steps[3:]), steps[1:3]
    mixed = exchange(plan, dict(zip(steps, found)), first)
    after = ()
    if later:
        after = delayed(plan, info, part(later, found), (wire, *part(first[1:], mixed)))
        mixed.update(exchange(plan, dict(zip(later, after)), later))
    if plan.group > 1:
        output = finish(plan, info, mixed, attended, gain, after[:1])
    else:
        output = finish_apart(plan, mixed, attended, gain)
    states = update(plan, info, states, spread(wire), False, (output,))
    return (output, *(jnp.transpose(w, (1, 2, 0)) for w in states))


def solution(mesh):
    tokens, state = P("tok", "head"), P("head", None, "tok")
    return jax.shard_map(
        on_device,
        mesh=mesh,
        in_specs=(tokens, tokens, tokens, tokens, P("tok"), P(), state, state, state, P("head")),
        out_specs=(tokens, state, state, state),
        check_vma=False,
    )
```
